256 devices in a mesh: outer: 16 (over z_hi, y), inner: 8 (over x, z_lo), section: 2 (over core).
Axes of the slice: x: 4, y: 4, z: 8 (z_hi: 4, z_lo: 2; z = z_hi * 2 + z_lo), core: 2. Of those that a mesh axis runs over, the one named last changes fastest.
Arguments:
- grad_out: bfloat16 [2, 16384, 2560], P('section', ('outer', 'inner')), may hold values from -6 to 6
- route_ids: int32 [2, 16384, 6], P('section', ('outer', 'inner')), may hold values from 0 to 127, as said below
- route_w: float32 [2, 16384, 6], P('section', ('outer', 'inner')), may hold values from 0.05 to 0.6
- saved: bfloat16 [2, 128, 896, 1536], P('section', ('outer', 'inner')), may hold values from -6 to 6
- w_up: bfloat16 [2, 128, 2560, 768], P('section', ('outer', 'inner')), may hold values from -0.125 to 0.125
- w_down: bfloat16 [2, 128, 768, 2560], P('section', ('outer', 'inner')), may hold values from -0.21875 to 0.21875
Outputs:
- input_grad: bfloat16 [2, 16384, 2560], P('section', ('outer', 'inner'))
- gate_grad: bfloat16 [2, 128, 896, 768], P('section', ('outer', 'inner'))
The draws below stay inside these ranges and needn't reach their ends.
Inputs may be any that keep to these rules, and one draw needn't show every extreme that they name: `route_ids`: each row names 6 different experts, 2 in each of 3 groups of 8 consecutive numbers; the routes of one group stand next to each other in route order. In each layer one expert is named by exactly 28 of the 128 rows of every index of outer and inner, and its group by no other rows.
All inputs are finite; a program needn't handle non-finite values.
Results may differ from the reference program's by a relative error of at most 0.012.
Values may be sent and summed in bfloat16 or wider, within the bound.
No kernel may reach another device: no remote copies, remote signals or barrier semaphores. Data moves between devices by JAX's collectives and lax.ppermute only.
A program may use at most 128 MiB of HBM per device.

```python
import math
import jax
import jax.numpy as jnp
from jax import lax

D = 2560
H = 768
TOP = 6
ROUTE_GROUPS = 3
TOK_DEV = 128
LAYERS = 2
GROUPS = 16
EXPERTS_IN_GROUP = 8
EXPERTS = 128
TOKENS = 16384
CAP = 7
GROUP_CAP = 28
SLOTS = 896
HOT_ROWS = 28


def draw_route_ids(key, part):
    first, second, third, fourth = jax.random.split(key, 4)
    hot_expert = jax.random.randint(first, (LAYERS,), 0, EXPERTS)
    popular_group = hot_expert // EXPERTS_IN_GROUP
    popular_inner_expert = hot_expert % EXPERTS_IN_GROUP
    order_scores = jax.random.randint(second, (LAYERS, EXPERTS, TOK_DEV), 0, 1 << 20) * TOK_DEV + jnp.arange(TOK_DEV, dtype=jnp.int32)
    positions = jnp.argsort(jnp.argsort(order_scores, axis=-1), axis=-1)
    popular_flag = (positions < HOT_ROWS).reshape(LAYERS, TOKENS)
    group_scores = jax.random.randint(third, (LAYERS, TOKENS, GROUPS), 0, 1 << 20) * GROUPS + jnp.arange(GROUPS, dtype=jnp.int32)
    at_hot = jnp.arange(GROUPS, dtype=jnp.int32)[None, None, :] == popular_group[:, None, None]
    group_scores = group_scores + jnp.where(popular_flag[:, :, None] & at_hot, 1 << 26, 0)
    group_scores = jnp.where(at_hot & jnp.logical_not(popular_flag[:, :, None]), -1, group_scores)
    unused, selected_groups = lax.top_k(group_scores, ROUTE_GROUPS)
    inner_expert_scores = jax.random.randint(fourth, (LAYERS, TOKENS, ROUTE_GROUPS, EXPERTS_IN_GROUP), 0, 1 << 20) * EXPERTS_IN_GROUP + jnp.arange(EXPERTS_IN_GROUP, dtype=jnp.int32)
    inner_score_boost = popular_flag[:, :, None, None] & (selected_groups[:, :, :, None] == popular_group[:, None, None, None]) & (jnp.arange(EXPERTS_IN_GROUP, dtype=jnp.int32)[None, None, None, :] == popular_inner_expert[:, None, None, None])
    inner_expert_scores = inner_expert_scores + jnp.where(inner_score_boost, 1 << 26, 0)
    unused_two, chosen_inner = lax.top_k(inner_expert_scores, TOP // ROUTE_GROUPS)
    chosen = selected_groups[:, :, :, None] * EXPERTS_IN_GROUP + chosen_inner
    return chosen.reshape(LAYERS, TOKENS, TOP).astype(jnp.int32)


def steps_of(rng, extent, cuts, low, largest):
    def one(position, parts):
        heights = jax.random.uniform(jax.random.fold_in(jax.random.fold_in(rng, 6), position), (parts,), jnp.float32, low / len(cuts), largest / len(cuts))
        return jnp.repeat(jnp.exp(heights), extent[position] // parts).reshape((-1,) + (1,) * (len(extent) - position - 1))

    factor_of = one(*cuts[0])
    for cut in cuts[1:]:
        factor_of = factor_of * one(*cut)
    return factor_of


def noise(own_key, extent, spread, most, shards=(), kind=jnp.bfloat16):
    loudness = steps_of(own_key, extent, shards, -0.22, 0.18) if shards else 1.0
    drawn = jax.random.normal(own_key, extent, jnp.float32) * spread * loudness
    return jnp.minimum(jnp.maximum(drawn, -most), most).astype(kind)


def setup_inputs(seed: int = 0) -> dict:
    seeds = jax.random.split(jax.random.key(seed), 7)
    return {
        "grad_out": noise(seeds[0], (LAYERS, TOKENS, D), 1.0, 6.0, ((0, 2), (1, 128))),
        "route_ids": draw_route_ids(jax.random.fold_in(seeds[6], 71), 0),
        "route_w": jnp.clip(jnp.exp(math.log(0.6) - 2.4849067 * jax.random.uniform(seeds[2], (LAYERS, TOKENS, TOP), jnp.float32) ** steps_of(seeds[2], (LAYERS, TOKENS, TOP), ((0, 2), (1, 128)), -0.2, 0.2)), 0.05, 0.6),
        "saved": noise(seeds[3], (LAYERS, EXPERTS, SLOTS, 2 * H), 1.0, 6.0, ((0, 2), (1, 128))),
        "w_up": noise(seeds[4], (LAYERS, EXPERTS, D, H), D ** -0.5, 0.125, ((0, 2), (1, 128))),
        "w_down": noise(seeds[5], (LAYERS, EXPERTS, H, D), H ** -0.5, 0.21875, ((0, 2), (1, 128))),
    }


def expert_pass(operands):
    rows, saved_one, up_one, down_one = operands
    hidden_grad = lax.dot_general(rows, down_one, (((1,), (1,)), ((), ())), preferred_element_type=jnp.float32)
    gate_act = saved_one[:, :H].astype(jnp.float32)
    up_value = saved_one[:, H:].astype(jnp.float32)
    up_grad = (hidden_grad * gate_act).astype(jnp.bfloat16)
    gate_grad = (hidden_grad * up_value).astype(jnp.bfloat16)
    input_rows = lax.dot_general(up_grad, up_one, (((1,), (1,)), ((), ())), preferred_element_type=jnp.float32)
    return input_rows.astype(jnp.bfloat16), gate_grad


def reference(grad_out, route_ids, route_w, saved, w_up, w_down):
    per_group = TOP // ROUTE_GROUPS
    token_grads = []
    gate_grads = []
    for layer in range(LAYERS):
        block_ids = route_ids[layer].reshape(EXPERTS, TOK_DEV, TOP).astype(jnp.int32)
        pair_group = block_ids[:, :, ::per_group] // EXPERTS_IN_GROUP
        group_hot = (pair_group[:, :, :, None] == jnp.arange(GROUPS, dtype=jnp.int32)[None, None, None, :]).astype(jnp.int32)
        token_groups = jnp.sum(group_hot, axis=2)
        earlier = jnp.cumsum(token_groups, axis=1) - token_groups
        group_rank = jnp.sum(earlier[:, :, None, :] * group_hot, axis=3)
        admitted = (group_rank < GROUP_CAP).astype(jnp.int32)
        route_adm = jnp.repeat(admitted, per_group, axis=2).reshape(EXPERTS, TOK_DEV * TOP)
        expert_ids = block_ids.reshape(EXPERTS, TOK_DEV * TOP)
        one_hot = (expert_ids[:, :, None] == jnp.arange(EXPERTS, dtype=jnp.int32)[None, None, :]).astype(jnp.int32) * route_adm[:, :, None]
        slot_rank = jnp.sum(jnp.cumsum(one_hot, axis=1) * one_hot, axis=2) - 1
        kept = (route_adm > 0) & (slot_rank < CAP)
        source = jnp.arange(EXPERTS, dtype=jnp.int32)[:, None]
        slot_index = jnp.where(kept, expert_ids * SLOTS + source * CAP + slot_rank, EXPERTS * SLOTS)
        slot_index = slot_index.reshape(-1).astype(jnp.int32)
        token_of = jnp.arange(TOKENS * TOP, dtype=jnp.int32) // TOP
        scaled = (grad_out[layer][token_of].astype(jnp.float32) * route_w[layer].reshape(-1)[:, None]).astype(jnp.bfloat16)
        dispatched = jnp.zeros((EXPERTS * SLOTS + 1, D), jnp.bfloat16).at[slot_index].set(scaled)
        dispatched = dispatched[:EXPERTS * SLOTS].reshape(EXPERTS, SLOTS, D)
        input_rows, gate_grad = lax.map(expert_pass, (dispatched, saved[layer], w_up[layer], w_down[layer]))
        flat_rows = jnp.concatenate([input_rows.reshape(EXPERTS * SLOTS, D), jnp.zeros((1, D), jnp.bfloat16)], axis=0)
        returned = flat_rows[slot_index].reshape(TOKENS, ROUTE_GROUPS, per_group, D)
        group_part = jnp.sum(returned.astype(jnp.float32), axis=2).astype(jnp.bfloat16)
        token_grads.append(jnp.sum(group_part.astype(jnp.float32), axis=1).astype(jnp.bfloat16))
        gate_grads.append(gate_grad)
    stacked = jnp.stack(token_grads, axis=0)
    input_grad = jnp.roll(stacked, -1, axis=0)
    return input_grad, jnp.stack(gate_grads, axis=0)
```

```python
import functools
import jax
import jax.numpy as jnp
from jax import lax
from jax.experimental import pallas as pl
from jax.experimental.pallas import tpu as pltpu
from jax.sharding import PartitionSpec as P

ROUTE_GROUPS = 3
F32 = jnp.float32
BF16 = jnp.bfloat16
I32 = jnp.int32
SUB = 8
TAIL = 256


def iota(shape, dim):
    return lax.broadcasted_iota(I32, shape, dim)


def dot(a, b):
    return lax.dot_general(a, b, (((1,), (0,)), ((), ())), preferred_element_type=F32)


def dot_t(a, b):
    return lax.dot_general(a, b, (((1,), (1,)), ((), ())), preferred_element_type=F32)


def flag(mask, kind=BF16):
    return jnp.where(mask, 1.0, 0.0).astype(kind)


def dispatch_kernel(dims, ids_ref, w_ref, g_ref, out_ref, rank_ref, lhs_ref, scale_ref, tails_ref):
    experts, tok, routes, in_group, group_cap, cap, main, width = dims
    step = pl.program_id(0)
    rows = experts * SUB

    @pl.when(step == 0)
    def _():
        e = iota((experts, tok), 0)
        named = jnp.zeros((experts, tok), F32)
        weight = jnp.zeros((experts, tok), F32)
        near = jnp.zeros((experts, tok), F32)
        for k in range(routes):
            ids = ids_ref[k : k + 1, :]
            hit = ids == e
            named += flag(hit, F32)
            weight += jnp.where(hit, w_ref[k : k + 1, :], 0.0)
            if k % (routes // ROUTE_GROUPS) == 0:
                near += flag(ids // in_group == e // in_group, F32)
        before = flag(iota((tok, tok), 0) < iota((tok, tok), 1))
        group_rank = dot(near.astype(BF16), before)
        admitted = (named > 0) & (group_rank < group_cap)
        slot_rank = dot(flag(admitted), before)
        rank = jnp.where(admitted & (slot_rank < cap), slot_rank, -1.0)
        rank_ref[...] = rank
        row = iota((rows, experts), 0)
        col = iota((rows, experts), 1)
        spread = flag(row // SUB == col)
        rank_rows = dot(spread, rank.astype(BF16))
        slot = flag(rank_rows == (iota((rows, tok), 0) % SUB).astype(F32), F32)
        high = weight.astype(BF16)
        rest = weight - high.astype(F32)
        mid = rest.astype(BF16)
        low = (rest - mid.astype(F32)).astype(BF16)
        weight_rows = (dot(spread, high) + dot(spread, mid)) + dot(spread, low)
        last = iota((rows, 1), 0) % SUB == SUB - 1
        scale_ref[...] = jnp.sum(slot * weight_rows, axis=1, keepdims=True) + flag(last, F32)
        lhs_ref[:, :tok] = slot.astype(BF16)
        lhs_ref[:, tok:] = flag((row // SUB == col) & (row % SUB == SUB - 1))
        g_tail = g_ref[:, main:]
        for j in range(main // TAIL):
            if j < cap:
                here = rank == float(j)
                w_slot = jnp.sum(jnp.where(here, weight, 0.0), axis=1, keepdims=True)
                tails_ref[:, j * TAIL : (j + 1) * TAIL] = (dot(flag(here), g_tail) * w_slot).astype(BF16)
            else:
                tails_ref[:, j * TAIL : (j + 1) * TAIL] = jnp.zeros((experts, TAIL), BF16)

    for j in range(width // TAIL):
        at = pl.ds(pl.multiple_of(step * width + j * TAIL, TAIL), TAIL)
        right = jnp.concatenate([g_ref[:, at], tails_ref[:, at]], axis=0)
        out_ref[:, j * TAIL : (j + 1) * TAIL] = (dot(lhs_ref[...], right) * scale_ref[...]).astype(BF16)


def picks_kernel(dims, ids_ref, rank_ref, pick_ref, pick_tail_ref):
    experts, tok, routes, parts = dims
    e = iota((experts, tok), 0)
    per = routes // ROUTE_GROUPS
    rows = experts * SUB
    spread = flag(iota((experts, rows), 0) == iota((experts, rows), 1) // SUB)
    lane = (iota((tok, rows), 1) % SUB).astype(F32)
    for j in range(ROUTE_GROUPS):
        hit = ids_ref[j * per : j * per + 1, :] == e
        for k in range(1, per):
            hit = hit | (ids_ref[j * per + k : j * per + k + 1, :] == e)
        rank = jnp.where(hit, rank_ref[...], -1.0).T
        pick_ref[j * tok : (j + 1) * tok, :] = flag(dot(rank.astype(BF16), spread) == lane)
        for r in range(parts):
            pick_tail_ref[r, j * tok : (j + 1) * tok, :] = flag(rank == float(r))


def expert_kernel(dims, a_ref, saved_ref, wd_ref, wu_ref, out_ref, gate_ref, place_ref, fetch_ref):
    rows, slots, cap, hidden, main = dims

    @pl.when(pl.program_id(0) == 0)
    def _():
        a, b = iota((rows, rows), 0), iota((rows, rows), 1)
        same = a // SUB == b // SUB
        for r in range(cap):
            place_ref[r] = flag(same & (a % SUB == SUB - 1) & (b % SUB == r))
            fetch_ref[r] = flag(same & (b % SUB == SUB - 1) & (a % SUB == r))

    tail = dot(fetch_ref[0], a_ref[:, :TAIL])
    for r in range(1, cap):
        tail += dot(fetch_ref[r], a_ref[:, r * TAIL : (r + 1) * TAIL])
    hidden_grad = dot_t(a_ref[...], wd_ref[:, :main]) + dot_t(tail.astype(BF16), wd_ref[:, main:])
    a, c = iota((rows, slots), 0), iota((rows, slots), 1)
    widen = flag((a % SUB < cap) & (c == a // SUB * cap + a % SUB))
    c, a = iota((slots, rows), 0), iota((slots, rows), 1)
    narrow = flag((a % SUB < cap) & (c == a // SUB * cap + a % SUB))
    gate_act = dot(widen, saved_ref[:, :hidden])
    up_grad = (hidden_grad * gate_act).astype(BF16)
    up_value = dot(widen, saved_ref[:, hidden:])
    gate_grad = (hidden_grad * up_value).astype(BF16)
    gate_ref[...] = dot(narrow, gate_grad).astype(BF16)
    tail = dot_t(up_grad, wu_ref[main:, :]).astype(BF16)
    for j in range(main // TAIL):
        part = dot_t(up_grad, wu_ref[j * TAIL : (j + 1) * TAIL, :])
        if j < cap:
            part += dot(place_ref[j], tail)
        out_ref[:, j * TAIL : (j + 1) * TAIL] = part.astype(BF16)


def combine_kernel(dims, pick_ref, pick_tail_ref, back_ref, out_ref, tail_ref):
    experts, tok, main, width, steps = dims
    step = pl.program_id(0)
    rows = experts * SUB

    def joined(part):
        part = part.astype(BF16).astype(F32)
        total = part[:tok]
        for j in range(1, ROUTE_GROUPS):
            total += part[j * tok : (j + 1) * tok]
        return total.astype(BF16)

    @pl.when(step == 0)
    def _():
        tail_ref[...] = jnp.zeros_like(tail_ref)

    lasts = flag(iota((experts, rows), 1) == iota((experts, rows), 0) * SUB + SUB - 1)
    for j in range(width // TAIL):
        block = back_ref[:, j * TAIL : (j + 1) * TAIL]
        at = pl.ds(pl.multiple_of(step * width + j * TAIL, TAIL), TAIL)
        out_ref[:, at] = joined(dot(pick_ref[...], block))
        tails = dot(lasts, block).astype(BF16)
        tail_ref[...] += dot(pick_tail_ref[step * (width // TAIL) + j], tails)

    @pl.when(step == steps - 1)
    def _():
        out_ref[:, main:] = joined(tail_ref[...])


def whole(shape):
    return pl.BlockSpec(shape, lambda *_: (0,) * len(shape), pipeline_mode=pl.Buffered(1))


def params(mib):
    return pltpu.CompilerParams(vmem_limit_bytes=mib * 2**20, dimension_semantics=("arbitrary",))


def cost(flops, moved):
    return pl.CostEstimate(flops=flops, bytes_accessed=moved, transcendentals=0)


def on_device(grad_out, route_ids, route_w, saved, w_up, w_down):
    groups_outer = lax.axis_size("outer")
    groups_inner = lax.axis_size("inner")
    experts = groups_outer * groups_inner
    tok, features = grad_out.shape[1:]
    routes = route_ids.shape[2]
    slots_all = saved.shape[2]
    cap = slots_all // experts
    hidden = w_up.shape[3]
    group_cap = max(2, 7 * tok * ROUTE_GROUPS // (6 * groups_outer))
    main = features - TAIL
    rows = experts * SUB
    steps = 3
    width = main // steps
    parts = main // TAIL
    ids = route_ids[0].T
    weights = route_w[0].T

    with jax.named_scope("dispatch"):
        outgoing, rank = pl.pallas_call(
            functools.partial(
                dispatch_kernel, (experts, tok, routes, groups_inner, group_cap, cap, main, width)
            ),
            grid=(steps,),
            in_specs=[whole((routes, tok)), whole((routes, tok)), whole((tok, features))],
            out_specs=[pl.BlockSpec((rows, width), lambda i: (0, i)), whole((experts, tok))],
            out_shape=[
                jax.ShapeDtypeStruct((rows, main), BF16),
                jax.ShapeDtypeStruct((experts, tok), F32),
            ],
            scratch_shapes=[
                pltpu.VMEM((rows, 2 * tok), BF16),
                pltpu.VMEM((rows, 1), F32),
                pltpu.VMEM((experts, main), BF16),
            ],
            compiler_params=params(24),
            cost_estimate=cost(2 * rows * 2 * tok * main, 2 * rows * main),
        )(ids, weights, grad_out[0])

    with jax.named_scope("picks"):
        pick, pick_tail = pl.pallas_call(
            functools.partial(picks_kernel, (experts, tok, routes, parts)),
            out_shape=[
                jax.ShapeDtypeStruct((ROUTE_GROUPS * tok, rows), BF16),
                jax.ShapeDtypeStruct((parts, ROUTE_GROUPS * tok, experts), BF16),
            ],
            compiler_params=pltpu.CompilerParams(vmem_limit_bytes=16 * 2**20),
            cost_estimate=cost(2 * ROUTE_GROUPS * tok * experts * rows, 4 * ROUTE_GROUPS * tok * rows),
        )(ids, rank)

    def exchange(block):
        moved = lax.all_to_all(
            block.reshape(experts, SUB, main), ("outer", "inner"), split_axis=0, concat_axis=0, tiled=True
        )
        return moved.reshape(rows, main)

    arrived = exchange(outgoing)

    with jax.named_scope("expert"):
        blocks = 4
        part, slots = rows // blocks, slots_all // blocks
        expert_rows, gate_grad = pl.pallas_call(
            functools.partial(expert_kernel, (part, slots, cap, hidden, main)),
            grid=(blocks,),
            in_specs=[
                pl.BlockSpec((part, main), lambda i: (i, 0)),
                pl.BlockSpec((slots, 2 * hidden), lambda i: (i, 0)),
                whole((hidden, features)),
                whole((features, hidden)),
            ],
            out_specs=[
                pl.BlockSpec((part, main), lambda i: (i, 0)),
                pl.BlockSpec((slots, hidden), lambda i: (i, 0)),
            ],
            out_shape=[
                jax.ShapeDtypeStruct((rows, main), BF16),
                jax.ShapeDtypeStruct((slots_all, hidden), BF16),
            ],
            scratch_shapes=[pltpu.VMEM((cap, part, part), BF16), pltpu.VMEM((cap, part, part), BF16)],
            compiler_params=params(40),
            cost_estimate=cost(4 * rows * features * hidden, 4 * (rows * main + features * hidden)),
        )(arrived, saved[0, 0], w_down[0, 0], w_up[0, 0])

    returned = exchange(expert_rows)

    with jax.named_scope("combine"):
        token_grad = pl.pallas_call(
            functools.partial(combine_kernel, (experts, tok, main, width, steps)),
            grid=(steps,),
            in_specs=[
                whole((ROUTE_GROUPS * tok, rows)),
                whole((parts, ROUTE_GROUPS * tok, experts)),
                pl.BlockSpec((rows, width), lambda i: (0, i)),
            ],
            out_specs=whole((tok, features)),
            out_shape=jax.ShapeDtypeStruct((tok, features), BF16),
            scratch_shapes=[pltpu.VMEM((ROUTE_GROUPS * tok, TAIL), F32)],
            compiler_params=params(24),
            cost_estimate=cost(2 * ROUTE_GROUPS * tok * rows * main, 2 * rows * main),
        )(pick, pick_tail, returned)

    count = lax.axis_size("section")
    received = lax.ppermute(token_grad, "section", [((i + 1) % count, i) for i in range(count)])
    return (received[None], gate_grad[None, None])


def solution(mesh):
    return jax.shard_map(
        on_device,
        mesh=mesh,
        in_specs=(
            P("section", ("outer", "inner"), None),
            P("section", ("outer", "inner"), None),
            P("section", ("outer", "inner"), None),
            P("section", ("outer", "inner"), None, None),
            P("section", ("outer", "inner"), None, None),
            P("section", ("outer", "inner"), None, None),
        ),
        out_specs=(
            P("section", ("outer", "inner"), None),
            P("section", ("outer", "inner"), None, None),
        ),
        check_vma=False,
    )
```

```python
import functools
import jax
import jax.numpy as jnp
from jax import lax
from jax.experimental import pallas as pl
from jax.experimental.pallas import tpu as pltpu
from jax.sharding import PartitionSpec as P

NZ, NY, NX = 8, 4, 4
ROUTE_GROUPS = 3
SUB = 8
SLABS = 3
FIELDS = 128
BLOCKS = 16
F32 = jnp.float32
BF16 = jnp.bfloat16
I32 = jnp.int32


def iota(shape, dim):
    return lax.broadcasted_iota(I32, shape, dim)


def dot(a, b):
    return lax.dot_general(a, b, (((1,), (0,)), ((), ())), preferred_element_type=F32)


def dot_t(a, b):
    return lax.dot_general(a, b, (((1,), (1,)), ((), ())), preferred_element_type=F32)


def t_dot(a, b):
    return lax.dot_general(a, b, (((0,), (0,)), ((), ())), preferred_element_type=F32)


def flag(mask, kind=BF16):
    return jnp.where(mask, 1.0, 0.0).astype(kind)


def over(value, divisor):
    return jnp.floor((value.astype(F32) + 0.5) * (1.0 / divisor)).astype(I32)


def top_bits(value):
    wide = value * 65537.0
    return wide - (wide - value)


def block_group(where_ref, block):
    odd, even, mid, far, y = (where_ref[i] for i in range(5))
    z = jnp.where(block < 4, odd, jnp.where(block < 8, even, jnp.where(block < 12, mid, far)))
    return (z // 2) * NY + jnp.where(block < 8, block % NY, (block + y) % NY)


def slots_in_group(member, group_cap):
    tok = member.shape[1]
    before = flag(iota((tok, tok), 0) < iota((tok, tok), 1))
    rank = dot(member.astype(BF16), before)
    return jnp.where((member > 0) & (rank < group_cap), rank, -1.0)


def token_lines(where_ref, group_slot):
    groups, tok = group_slot.shape
    rows = (SLABS + 1) * BLOCKS * SUB
    r = iota((rows, groups), 0)
    chosen = flag(block_group(where_ref, (r // SUB) % BLOCKS) == iota((rows, groups), 1))
    r = iota((rows, tok), 0)
    slab, sub = r // (BLOCKS * SUB), r % SUB
    slot = jnp.where(slab == SLABS, SLABS * SUB + sub % 4, slab * SUB + sub)
    return flag(dot(chosen, group_slot.astype(BF16)) == slot.astype(F32))


def half_rows(value, second):
    sub = iota(value.shape, 0) % SUB
    return jnp.where(sub >= 4 if second else sub < 4, value, jnp.zeros_like(value))


def half_right(block_ref, second):
    features = block_ref.shape[1] // (2 * SLABS + 1) // FIELDS * FIELDS * 2
    half, tail = features // 2, SLABS * features
    c = half if second else 0
    last = half_rows(block_ref[:, tail : tail + half].astype(F32), second).astype(BF16)
    return jnp.concatenate([*(block_ref[:, n * features + c : n * features + c + half] for n in range(SLABS)), last], axis=0)


def lines_kernel(dims, where_ref, ids_ref, line_ref):
    groups, in_group, group_cap = dims
    routes, _, tok = ids_ref.shape
    member = jnp.zeros((groups, tok), F32)
    for k in range(0, routes, routes // ROUTE_GROUPS):
        member += flag(ids_ref[k] // in_group == iota((groups, tok), 0), F32)
    line_ref[...] = token_lines(where_ref, slots_in_group(member, group_cap))


def put_blocks(block_refs, value, start):
    value, row = value.astype(BF16), 0
    for ref in block_refs:
        ref[:, start : start + value.shape[1]] = value[row : row + ref.shape[0]]
        row += ref.shape[0]


def stack_blocks(block_refs, stacked_ref):
    width, row, first = stacked_ref.shape[1], 0, None
    for ref in block_refs:
        if ref.shape[0] > SUB:
            stacked_ref[row : row + ref.shape[0], :] = ref[:, :width]
            row += ref.shape[0]
        elif first is None:
            first = ref
        else:
            pair = jnp.concatenate([first[:, :width].astype(F32), ref[:, :width].astype(F32)], axis=0)
            stacked_ref[row : row + 2 * SUB, :] = pair.astype(BF16)
            row, first = row + 2 * SUB, None


def dispatch_kernel(dims, where_ref, ids_ref, w_ref, g_ref, *block_refs):
    groups, in_group, group_cap, cap = dims
    routes, _, tok = ids_ref.shape
    features, experts = g_ref.shape[1], groups * in_group
    half, per = features // 2, routes // ROUTE_GROUPS
    e, group = iota((experts, tok), 0), iota((groups, tok), 0)
    before = flag(iota((tok, tok), 0) < iota((tok, tok), 1))
    ids = [ids_ref[k] for k in range(routes)]
    named = jnp.zeros((experts, tok), F32)
    mine = jnp.zeros((experts, tok), F32)
    member = jnp.zeros((groups, tok), F32)
    for k in range(routes):
        named += flag(ids[k] == e, F32)
        if k % per == 0:
            mine += flag(ids[k] // in_group == e // in_group, F32)
            member += flag(ids[k] // in_group == group, F32)
    admitted = (named > 0) & (dot(mine.astype(BF16), before) < group_cap)
    slot_rank = dot(flag(admitted), before)
    rank = jnp.where(admitted & (slot_rank < cap), slot_rank, -1.0)
    group_slot = slots_in_group(member, group_cap)
    fields = [jnp.zeros((groups, tok), F32) for _ in range(SUB)]
    for k in range(routes):
        own = jnp.sum(jnp.where(ids[k] == e, rank, 0.0), axis=0, keepdims=True)
        place = jnp.where(own >= 0, (ids[k] % in_group).astype(F32) * cap + own + 1.0, 0.0)
        weight = w_ref[k]
        first = top_bits(weight)
        second = top_bits(weight - first)
        third = (weight - first) - second
        at = ids[k] // in_group == group
        for f, value in ((k % per, place), *((per + 3 * (k % per) + i, v) for i, v in enumerate((first, second, third)))):
            fields[f] += jnp.where(at, value, 0.0)
    stacked = jnp.concatenate([f.astype(BF16) for f in fields], axis=0)
    line = token_lines(where_ref, group_slot)
    rows, part = line.shape[0], groups * SUB
    r, c = iota((part, part), 0), iota((part, part), 1)
    choose = flag((block_group(where_ref, r // SUB) == c % groups) & (r % SUB == c // groups))
    by_block = dot(choose, stacked).astype(BF16)
    by_slot = dot_t(by_block, line)
    r, c = iota((part, rows), 0), iota((part, rows), 1)
    by_slot = jnp.where((c // SUB) % groups == r // SUB, by_slot, 0.0).astype(BF16)
    r, c = iota((rows, FIELDS), 0), iota((rows, FIELDS), 1)
    fold = flag(c == (r // part) * SUB + r % SUB)
    block_fields = dot(by_slot, fold)

    def put(value, start, width):
        put_blocks(block_refs, value, start)

    for n in range(SLABS):
        for c in (0, half):
            put(dot(line[n * part : (n + 1) * part], g_ref[:, c : c + half]), n * features + c, half)
    line = line[SLABS * part :]
    put(
        half_rows(dot(line, g_ref[:, :half]), False) + half_rows(dot(line, g_ref[:, half:]), True),
        SLABS * features, half,
    )
    put(block_fields, SLABS * features + half, FIELDS)


def spread_kernel(dims, *refs):
    *block_refs, out_hbm, hit_ref, block_ref, out_ref, sems = refs
    stack_blocks(block_refs, block_ref)
    in_group, cap = dims
    height, features = block_ref.shape[0], out_ref.shape[1]
    sources = height // SUB
    half, tail = features // 2, SLABS * features

    deep = (SLABS + 1) * height
    l, c = iota((FIELDS, deep), 0), iota((FIELDS, deep), 1)
    unfold = flag((l == (c // height) * SUB + c % SUB) & (l < (SLABS + 1) * SUB))
    wide = dot(block_ref[:, tail + half :], unfold)
    r, c = iota((height, deep), 0), iota((height, deep), 1)
    wide = jnp.where(r // SUB == (c // SUB) % sources, wide, 0.0)
    fields = wide[:SUB]
    for q in range(1, sources):
        fields += wide[q * SUB : (q + 1) * SUB]
    places = [fields[k : k + 1].astype(I32) for k in range(2)]
    weights = [(fields[2 + 3 * k : 3 + 3 * k] + fields[3 + 3 * k : 4 + 3 * k]) + fields[4 + 3 * k : 5 + 3 * k] for k in range(2)]
    rows = out_ref.shape[0]
    s = iota((rows, 1), 0)
    each = rows // in_group
    expert = over(s, each)
    inside = s - expert * each
    source = over(inside, cap)
    key = source * 64 + expert * cap + (inside - source * cap) + 1
    key = jnp.where(source < sources, key, -2)
    c = iota((1, deep), 1)
    base = ((c // SUB) % sources) * 64
    hits = [key == jnp.where(place > 0, base + place, -1) for place in places]
    once = iota((1, deep), 1)
    once = (once < SLABS * height) | (once % SUB < 4)
    hit_ref[...] = flag(hits[0] | hits[1])
    scale = jnp.where(hits[0], jnp.where(once, weights[0], 0.0), 0.0)
    scale += jnp.where(hits[1], jnp.where(once, weights[1], 0.0), 0.0)
    scale = jnp.sum(scale, axis=1, keepdims=True)
    copies = []
    for c in (0, half):
        out_ref[:, c : c + half] = (dot(hit_ref[...], half_right(block_ref, c > 0)) * scale).astype(BF16)
        copies.append(
            pltpu.make_async_copy(out_ref.at[:, pl.ds(c, half)], out_hbm.at[:, pl.ds(c, half)], sems.at[c // half])
        )
        copies[-1].start()
    for copy in copies:
        copy.wait()


def gather_kernel(rows_hbm, hit_ref, *refs):
    *block_refs, rows_ref, sems = refs
    features, height = rows_ref.shape[1], hit_ref.shape[1] // (SLABS + 1)
    half = features // 2
    copies = [
        pltpu.make_async_copy(rows_hbm.at[:, pl.ds(c, half)], rows_ref.at[:, pl.ds(c, half)], sems.at[c // half])
        for c in (0, half)
    ]
    for copy in copies:
        copy.start()
    tail = jnp.zeros((height, half), F32)
    for copy, c in zip(copies, (0, half), strict=True):
        copy.wait()
        got = t_dot(hit_ref[...], rows_ref[:, c : c + half])
        for n in range(SLABS):
            put_blocks(block_refs, got[n * height : (n + 1) * height], n * features + c)
        tail += half_rows(got[SLABS * height :], c > 0)
    put_blocks(block_refs, tail, SLABS * features)


def combine_kernel(*refs):
    *block_refs, line_ref, out_ref, block_ref = refs
    stack_blocks(block_refs, block_ref)
    half = out_ref.shape[1] // 2
    for c in (0, half):
        out_ref[:, c : c + half] = t_dot(line_ref[...], half_right(block_ref, c > 0)).astype(BF16)


def true_rows(where_ref, row, part, each, cap):
    y, z_hi = where_ref[4], where_ref[5]
    sender = over(row, each)
    inside = row - sender * each
    q = over(inside, cap)
    slot = inside - q * cap
    z = z_hi * 2 + sender % 2
    up = jnp.where(sender % 2 == 1, 1, -1)
    if part == 0:
        sources = 12
        odd = jnp.where(sender % 2 == 1, z, z - 1)
        z = jnp.where(q < 4, odd, jnp.where(q < 8, odd + 1, z + 2 * up))
        at_y = jnp.where(q < 8, q, y - q + 4 * NY)
    else:
        sources = 4
        z = z + 3 * up
        at_y = y - q + 4 * NY
    z = (z + NZ) % NZ
    source = (((z // 2) * NY + at_y % NY) * NX + sender // 2) * 2 + z % 2
    return jnp.where(q < sources, source * cap + slot, -1)


def align_kernel(dims, where_ref, saved_ref, *part_refs):
    in_group, cap = dims
    slots = saved_ref.shape[0]
    for part, ref in enumerate(part_refs):
        rows = ref.shape[0]
        true = true_rows(where_ref, iota((rows, 1), 0), part, rows // in_group, cap)
        ref[...] = dot(flag(true == iota((rows, slots), 1)), saved_ref[...]).astype(BF16)


def restore_kernel(dims, where_ref, *refs):
    in_group, cap = dims
    *part_refs, out_ref = refs
    slots = out_ref.shape[0]
    total = jnp.zeros(out_ref.shape, F32)
    for part, ref in enumerate(part_refs):
        rows = ref.shape[0]
        true = true_rows(where_ref, iota((1, rows), 1), part, rows // in_group, cap)
        total += dot(flag(true == iota((slots, rows), 0)), ref[...])
    out_ref[...] = total.astype(BF16)


def expert_kernel(x_hbm, kept_hbm, wd_hbm, wu_hbm, out_hbm, gate_hbm, x_ref, kept_ref, wd_ref, wu_ref, up_ref, out_ref, gate_ref, sems):
    hidden, features = wd_ref.shape
    rows = x_ref.shape[0]
    step, wide, tall = hidden // 3, features // 5, rows // 2 if rows > 256 else rows
    count = iter(range(sems.shape[0]))

    def copy(source, target, index):
        return pltpu.make_async_copy(source.at[index], target.at[index], sems.at[next(count)])

    tops = [pl.ds(r, tall) for r in range(0, rows, tall)]
    x = [copy(x_hbm, x_ref, t) for t in tops]
    kept = [copy(kept_hbm, kept_ref, t) for t in tops]
    down = [copy(wd_hbm, wd_ref, pl.ds(n, step)) for n in range(0, hidden, step)]
    up = [copy(wu_hbm, wu_ref, pl.ds(n, wide)) for n in range(0, features, wide)]
    for c in (x[0], down[0], kept[0], *down[1:], *x[1:], *kept[1:], *up):
        c.start()
    out = []
    for i, r in enumerate(range(0, rows, tall)):
        x[i].wait()
        for j, n in enumerate(range(0, hidden, step)):
            if i == 0:
                down[j].wait()
            grad = dot_t(x_ref[r : r + tall, :], wd_ref[n : n + step, :])
            if j == 0:
                kept[i].wait()
            act = kept_ref[r : r + tall, n : n + step].astype(F32)
            up_ref[r : r + tall, n : n + step] = (grad * act).astype(BF16)
            value = kept_ref[r : r + tall, hidden + n : hidden + n + step].astype(F32)
            gate_ref[r : r + tall, n : n + step] = (grad * value).astype(BF16)
        out.append(copy(gate_ref, gate_hbm, tops[i]))
        out[-1].start()
    for i, n in enumerate(range(0, features, wide)):
        up[i].wait()
        out_ref[:, n : n + wide] = dot_t(up_ref[...], wu_ref[n : n + wide, :]).astype(BF16)
        out.append(copy(out_ref, out_hbm, (slice(None), pl.ds(n, wide))))
        out[-1].start()
    for c in out:
        c.wait()


def device_at(z, y, x):
    return (((z // 2) % (NZ // 2) * NY + y % NY) * NX + x) * 2 + z % 2


PAIR_SETS = [
    [device_at(z % NZ, y, x) for z in (odd, odd + 1) for y in range(NY)]
    for x in range(NX)
    for odd in range(1, NZ, 2)
]


def routes_over(hops, dy, back):
    pairs = []
    for z in range(NZ):
        to = (z + (hops if (z % 2 == 1) == (hops == 3) else -hops)) % NZ
        pairs += [(device_at(z, y, x), device_at(to, y + dy, x)) for y in range(NY) for x in range(NX)]
    return [(b, a) for a, b in pairs] if back else pairs


def on_device(grad_out, route_ids, route_w, saved, w_up, w_down):
    both = ("outer", "inner")
    groups, in_group = lax.axis_size("outer"), lax.axis_size("inner")
    tok, features = grad_out.shape[1:]
    routes = route_ids.shape[2]
    slots_all = saved.shape[2]
    cap = slots_all // (groups * in_group)
    hidden = w_up.shape[3]
    group_cap = max(2, 7 * tok * ROUTE_GROUPS // (6 * groups))
    wide = SLABS * features + features // 2
    sent = wide + FIELDS
    deep = (SLABS + 1) * BLOCKS * SUB
    heights = [in_group * -(-(sources * cap) // SUB) * SUB for sources in (12, 4)]
    outer, inner = lax.axis_index("outer"), lax.axis_index("inner")
    z_hi, y, z_lo = outer // NY, outer % NY, inner % 2
    z = z_hi * 2 + z_lo
    up = 2 * z_lo - 1
    odd = (z + z_lo - 1) % NZ
    where = jnp.stack([odd, (odd + 1) % NZ, (z - 2 * up) % NZ, (z + 3 * up) % NZ, y, z_hi]).astype(I32)
    vmem, hbm = pl.BlockSpec(memory_space=pltpu.VMEM), pl.BlockSpec(memory_space=pltpu.HBM)
    smem = pl.BlockSpec(memory_space=pltpu.SMEM)

    def array(*shape):
        return jax.ShapeDtypeStruct(shape, BF16)

    def call(kernel, name, n_in, outs, mib, flops, out_specs=None, scratch=(), scalars=True):
        moved = 2 * sum(functools.reduce(lambda a, b: a * b, o.shape) for o in outs)
        return pl.pallas_call(
            kernel,
            name=name,
            in_specs=[smem] * scalars + [vmem] * n_in,
            out_specs=out_specs or [vmem] * len(outs),
            out_shape=list(outs),
            scratch_shapes=list(scratch),
            compiler_params=pltpu.CompilerParams(vmem_limit_bytes=mib * 2**20),
            cost_estimate=pl.CostEstimate(flops=flops, bytes_accessed=moved, transcendentals=0),
        )

    def near_swap(block):
        width = block.shape[1]
        moved = lax.all_to_all(block.reshape(8, SUB, width), both, 0, 0, axis_index_groups=PAIR_SETS, tiled=True)
        return moved.reshape(8 * SUB, width)

    def hop(blocks, hops, back=False):
        return [lax.ppermute(b, both, routes_over(hops, dy, back)) for dy, b in enumerate(blocks)]

    def in_groups(rows):
        moved = lax.all_to_all(rows.reshape(in_group, -1, features), "inner", 0, 0, tiled=True)
        return moved.reshape(rows.shape)

    def spread(name, blocks, rows):
        height = sum(b.shape[0] for b in blocks)
        depth = (SLABS + 1) * height
        return call(
            functools.partial(spread_kernel, (in_group, cap)), name, len(blocks),
            [array(rows, features), array(rows, depth)], 48, 2 * rows * depth * features,
            [hbm, vmem],
            [pltpu.VMEM((height, sent), BF16), pltpu.VMEM((rows, features), BF16), pltpu.SemaphoreType.DMA((2,))],
            scalars=False,
        )(*blocks)

    def gather(name, rows, hit, shapes):
        return pl.pallas_call(
            gather_kernel,
            name=name,
            in_specs=[hbm, vmem],
            out_specs=[vmem] * len(shapes),
            out_shape=[array(h, wide) for h in shapes],
            scratch_shapes=[pltpu.VMEM(rows.shape, BF16), pltpu.SemaphoreType.DMA((2,))],
            compiler_params=pltpu.CompilerParams(vmem_limit_bytes=20 * 2**20),
            cost_estimate=pl.CostEstimate(
                flops=2 * hit.shape[0] * hit.shape[1] * features, bytes_accessed=2 * rows.shape[0] * features, transcendentals=0
            ),
        )(rows, hit)

    def after(first, *values):
        *values, first = lax.optimization_barrier((*values, first))
        return first, *values

    ids = route_ids[0].T.reshape(routes, 1, tok)
    shapes = [8 * SUB] + [SUB] * 8
    near, *others = call(
        functools.partial(dispatch_kernel, (groups, in_group, group_cap, cap)), "dispatch", 3,
        [array(h, sent) for h in shapes], 12, 2 * deep * tok * features,
    )(where, ids, route_w[0].T.reshape(routes, 1, tok), grad_out[0])
    [line] = call(
        functools.partial(lines_kernel, (groups, in_group, group_cap)), "lines", 1,
        [array(deep, tok)], 8, 4 * deep * tok * tok,
    )(where, ids)
    kept = call(
        functools.partial(align_kernel, (in_group, cap)), "align", 1, [array(h, 2 * hidden) for h in heights], 16,
        4 * sum(heights) * slots_all * hidden,
    )(where, saved[0, 0])

    near, mid, far = near_swap(near), hop(others[:4], 2), others[4:]
    near, *ready = after(near, *mid, *far)
    mid, far = ready[:4], hop(ready[4:], 3)
    rows_n, hit_n = spread("spread_near", [near, *mid], heights[0])
    rows_n = in_groups(rows_n)
    rows_f, hit_f = spread("spread_far", far, heights[1])
    rows_n, rows_f = after(rows_n, rows_f)
    rows_f = in_groups(rows_f)
    rows_n, gate_n = expert_call("expert_near", rows_n, kept[0], w_down[0, 0], w_up[0, 0])
    rows_f, gate_f = expert_call("expert_far", rows_f, kept[1], w_down[0, 0], w_up[0, 0])
    rows_f = in_groups(rows_f)
    far = gather("gather_far", rows_f, hit_f, [SUB] * 4)
    rows_n, *far = after(rows_n, *far)
    far = hop(far, 3, True)
    rows_n = in_groups(rows_n)
    rows_n, *far = after(rows_n, *far)
    [gate_grad] = call(
        functools.partial(restore_kernel, (in_group, cap)), "restore", 2, [array(slots_all, hidden)], 12,
        2 * sum(heights) * slots_all * hidden,
    )(where, gate_n, gate_f)
    near, *mid = gather("gather_near", rows_n, hit_n, [8 * SUB] + [SUB] * 4)
    near, mid = near_swap(near), hop(mid, 2, True)
    gate_grad, line = after(gate_grad, line)
    [token_grad] = call(
        combine_kernel, "combine", 10, [array(tok, features)], 12, 2 * deep * tok * features,
        scratch=[pltpu.VMEM((BLOCKS * SUB, wide), BF16)], scalars=False,
    )(near, *mid, *far, line)
    count = lax.axis_size("section")
    received = lax.ppermute(token_grad, "section", [((i + 1) % count, i) for i in range(count)])
    return (received[None], gate_grad[None, None])


def expert_call(name, rows, kept, w_down, w_up):
    hidden, features = w_down.shape
    height = rows.shape[0]
    hbm = pl.BlockSpec(memory_space=pltpu.HBM)
    return pl.pallas_call(
        expert_kernel,
        name=name,
        in_specs=[hbm] * 4,
        out_specs=[hbm] * 2,
        out_shape=[jax.ShapeDtypeStruct((height, features), BF16), jax.ShapeDtypeStruct((height, hidden), BF16)],
        scratch_shapes=[
            pltpu.VMEM((height, features), BF16),
            pltpu.VMEM((height, 2 * hidden), BF16),
            pltpu.VMEM((hidden, features), BF16),
            pltpu.VMEM((features, hidden), BF16),
            pltpu.VMEM((height, hidden), BF16),
            pltpu.VMEM((height, features), BF16),
            pltpu.VMEM((height, hidden), BF16),
            pltpu.SemaphoreType.DMA((19,)),
        ],
        compiler_params=pltpu.CompilerParams(vmem_limit_bytes=56 * 2**20),
        cost_estimate=pl.CostEstimate(
            flops=4 * height * features * hidden, bytes_accessed=4 * (height + hidden) * features, transcendentals=0
        ),
    )(rows, kept, w_down, w_up)


def solution(mesh):
    return jax.shard_map(
        on_device,
        mesh=mesh,
        in_specs=(
            P("section", ("outer", "inner"), None),
            P("section", ("outer", "inner"), None),
            P("section", ("outer", "inner"), None),
            P("section", ("outer", "inner"), None, None),
            P("section", ("outer", "inner"), None, None),
            P("section", ("outer", "inner"), None, None),
        ),
        out_specs=(
            P("section", ("outer", "inner"), None),
            P("section", ("outer", "inner"), None, None),
        ),
        check_vma=False,
    )
```

```python
import functools
import jax
import jax.numpy as jnp
from jax import lax
from jax.experimental import pallas as pl
from jax.experimental.pallas import tpu as pltpu
from jax.sharding import PartitionSpec as P

NZ, NY, NX = 8, 4, 4
ROUTE_GROUPS = 3
SUB = 8
SLABS = 3
FIELDS = 128
BLOCKS = 16
F32 = jnp.float32
BF16 = jnp.bfloat16
I32 = jnp.int32


def iota(shape, dim):
    return lax.broadcasted_iota(I32, shape, dim)


def dot(a, b):
    return lax.dot_general(a, b, (((1,), (0,)), ((), ())), preferred_element_type=F32)


def dot_t(a, b):
    return lax.dot_general(a, b, (((1,), (1,)), ((), ())), preferred_element_type=F32)


def t_dot(a, b):
    return lax.dot_general(a, b, (((0,), (0,)), ((), ())), preferred_element_type=F32)


def flag(mask, kind=BF16):
    return jnp.where(mask, 1.0, 0.0).astype(kind)


def over(value, divisor):
    return jnp.floor((value.astype(F32) + 0.5) * (1.0 / divisor)).astype(I32)


def top_bits(value):
    wide = value * 65537.0
    return wide - (wide - value)


def block_group(where_ref, block):
    odd, even, mid, far, y = (where_ref[i] for i in range(5))
    z = jnp.where(block < 4, odd, jnp.where(block < 8, even, jnp.where(block < 12, mid, far)))
    return (z // 2) * NY + jnp.where(block < 8, block % NY, (block + y) % NY)


def slots_in_group(member, group_cap):
    tok = member.shape[1]
    before = flag(iota((tok, tok), 0) < iota((tok, tok), 1))
    rank = dot(member.astype(BF16), before)
    return jnp.where((member > 0) & (rank < group_cap), rank, -1.0)


def token_lines(where_ref, group_slot):
    groups, tok = group_slot.shape
    rows = (SLABS + 1) * BLOCKS * SUB
    r = iota((rows, groups), 0)
    chosen = flag(block_group(where_ref, (r // SUB) % BLOCKS) == iota((rows, groups), 1))
    r = iota((rows, tok), 0)
    slab, sub = r // (BLOCKS * SUB), r % SUB
    slot = jnp.where(slab == SLABS, SLABS * SUB + sub % 4, slab * SUB + sub)
    return flag(dot(chosen, group_slot.astype(BF16)) == slot.astype(F32))


def half_rows(value, second):
    sub = iota(value.shape, 0) % SUB
    return jnp.where(sub >= 4 if second else sub < 4, value, jnp.zeros_like(value))


def half_right(block_ref, second):
    features = block_ref.shape[1] // (2 * SLABS + 1) // FIELDS * FIELDS * 2
    half, tail = features // 2, SLABS * features
    c = half if second else 0
    last = half_rows(block_ref[:, tail : tail + half].astype(F32), second).astype(BF16)
    return jnp.concatenate([*(block_ref[:, n * features + c : n * features + c + half] for n in range(SLABS)), last], axis=0)


def lines_kernel(dims, where_ref, ids_ref, line_ref):
    groups, in_group, group_cap = dims
    routes, _, tok = ids_ref.shape
    member = jnp.zeros((groups, tok), F32)
    for k in range(0, routes, routes // ROUTE_GROUPS):
        member += flag(ids_ref[k] // in_group == iota((groups, tok), 0), F32)
    line_ref[...] = token_lines(where_ref, slots_in_group(member, group_cap))


def put_blocks(block_refs, value, start):
    row = 0
    for ref in block_refs:
        ref[:, start : start + value.shape[1]] = value[row : row + ref.shape[0]].astype(BF16)
        row += ref.shape[0]


def stack_blocks(block_refs, stacked_ref):
    width, row, first = stacked_ref.shape[1], 0, None
    for ref in block_refs:
        if ref.shape[0] > SUB:
            stacked_ref[row : row + ref.shape[0], :] = ref[:, :width]
            row += ref.shape[0]
        elif first is None:
            first = ref
        else:
            pair = jnp.concatenate([first[:, :width].astype(F32), ref[:, :width].astype(F32)], axis=0)
            stacked_ref[row : row + 2 * SUB, :] = pair.astype(BF16)
            row, first = row + 2 * SUB, None


def dispatch_kernel(dims, where_ref, ids_ref, w_ref, g_ref, *block_refs):
    groups, in_group, group_cap, cap = dims
    routes, _, tok = ids_ref.shape
    features, experts = g_ref.shape[1], groups * in_group
    half, per = features // 2, routes // ROUTE_GROUPS
    e, group = iota((experts, tok), 0), iota((groups, tok), 0)
    before = flag(iota((tok, tok), 0) < iota((tok, tok), 1))
    ids = [ids_ref[k] for k in range(routes)]
    named = jnp.zeros((experts, tok), F32)
    mine = jnp.zeros((experts, tok), F32)
    member = jnp.zeros((groups, tok), F32)
    for k in range(routes):
        named += flag(ids[k] == e, F32)
        if k % per == 0:
            mine += flag(ids[k] // in_group == e // in_group, F32)
            member += flag(ids[k] // in_group == group, F32)
    admitted = (named > 0) & (dot(mine.astype(BF16), before) < group_cap)
    slot_rank = dot(flag(admitted), before)
    rank = jnp.where(admitted & (slot_rank < cap), slot_rank, -1.0)
    group_slot = slots_in_group(member, group_cap)
    fields = [jnp.zeros((groups, tok), F32) for _ in range(SUB)]
    for k in range(routes):
        own = jnp.sum(jnp.where(ids[k] == e, rank, 0.0), axis=0, keepdims=True)
        place = jnp.where(own >= 0, (ids[k] % in_group).astype(F32) * cap + own + 1.0, 0.0)
        weight = w_ref[k]
        first = top_bits(weight)
        second = top_bits(weight - first)
        third = (weight - first) - second
        at = ids[k] // in_group == group
        for f, value in ((k % per, place), *((per + 3 * (k % per) + i, v) for i, v in enumerate((first, second, third)))):
            fields[f] += jnp.where(at, value, 0.0)
    stacked = jnp.concatenate([f.astype(BF16) for f in fields], axis=0)
    line = token_lines(where_ref, group_slot)
    rows, part = line.shape[0], groups * SUB
    r, c = iota((part, part), 0), iota((part, part), 1)
    choose = flag((block_group(where_ref, r // SUB) == c % groups) & (r % SUB == c // groups))
    by_block = dot(choose, stacked).astype(BF16)
    by_slot = dot_t(by_block, line)
    r, c = iota((part, rows), 0), iota((part, rows), 1)
    by_slot = jnp.where((c // SUB) % groups == r // SUB, by_slot, 0.0).astype(BF16)
    r, c = iota((rows, FIELDS), 0), iota((rows, FIELDS), 1)
    fold = flag(c == (r // part) * SUB + r % SUB)
    block_fields = dot(by_slot, fold)

    def put(value, start, width):
        put_blocks(block_refs, value, start)

    for n in range(SLABS):
        for c in (0, half):
            put(dot(line[n * part : (n + 1) * part], g_ref[:, c : c + half]), n * features + c, half)
    line = line[SLABS * part :]
    put(
        half_rows(dot(line, g_ref[:, :half]), False) + half_rows(dot(line, g_ref[:, half:]), True),
        SLABS * features, half,
    )
    put(block_fields, SLABS * features + half, FIELDS)


def spread_kernel(dims, *refs):
    *block_refs, out_hbm, hit_ref, block_ref, out_ref, sems = refs
    stack_blocks(block_refs, block_ref)
    in_group, cap = dims
    height, features = block_ref.shape[0], out_ref.shape[1]
    sources = height // SUB
    half, tail = features // 2, SLABS * features

    deep = (SLABS + 1) * height
    l, c = iota((FIELDS, deep), 0), iota((FIELDS, deep), 1)
    unfold = flag((l == (c // height) * SUB + c % SUB) & (l < (SLABS + 1) * SUB))
    wide = dot(block_ref[:, tail + half :], unfold)
    r, c = iota((height, deep), 0), iota((height, deep), 1)
    wide = jnp.where(r // SUB == (c // SUB) % sources, wide, 0.0)
    fields = wide[:SUB]
    for q in range(1, sources):
        fields += wide[q * SUB : (q + 1) * SUB]
    places = [fields[k : k + 1].astype(I32) for k in range(2)]
    weights = [(fields[2 + 3 * k : 3 + 3 * k] + fields[3 + 3 * k : 4 + 3 * k]) + fields[4 + 3 * k : 5 + 3 * k] for k in range(2)]
    rows = out_ref.shape[0]
    s = iota((rows, 1), 0)
    each = rows // in_group
    expert = over(s, each)
    inside = s - expert * each
    source = over(inside, cap)
    key = source * 64 + expert * cap + (inside - source * cap) + 1
    key = jnp.where(source < sources, key, -2)
    c = iota((1, deep), 1)
    base = ((c // SUB) % sources) * 64
    hits = [key == jnp.where(place > 0, base + place, -1) for place in places]
    once = iota((1, deep), 1)
    once = (once < SLABS * height) | (once % SUB < 4)
    hit_ref[...] = flag(hits[0] | hits[1])
    scale = jnp.where(hits[0], jnp.where(once, weights[0], 0.0), 0.0)
    scale += jnp.where(hits[1], jnp.where(once, weights[1], 0.0), 0.0)
    scale = jnp.sum(scale, axis=1, keepdims=True)
    copies = []
    for c in (0, half):
        out_ref[:, c : c + half] = (dot(hit_ref[...], half_right(block_ref, c > 0)) * scale).astype(BF16)
        copies.append(
            pltpu.make_async_copy(out_ref.at[:, pl.ds(c, half)], out_hbm.at[:, pl.ds(c, half)], sems.at[c // half])
        )
        copies[-1].start()
    for copy in copies:
        copy.wait()


def gather_kernel(rows_hbm, hit_ref, *refs):
    *block_refs, rows_ref, sems = refs
    features, height = rows_ref.shape[1], hit_ref.shape[1] // (SLABS + 1)
    half = features // 2
    copies = [
        pltpu.make_async_copy(rows_hbm.at[:, pl.ds(c, half)], rows_ref.at[:, pl.ds(c, half)], sems.at[c // half])
        for c in (0, half)
    ]
    for copy in copies:
        copy.start()
    tail = jnp.zeros((height, half), F32)
    for copy, c in zip(copies, (0, half), strict=True):
        copy.wait()
        got = t_dot(hit_ref[...], rows_ref[:, c : c + half])
        for n in range(SLABS):
            put_blocks(block_refs, got[n * height : (n + 1) * height], n * features + c)
        tail += half_rows(got[SLABS * height :], c > 0)
    put_blocks(block_refs, tail, SLABS * features)


def combine_kernel(*refs):
    *block_refs, line_ref, out_ref, block_ref = refs
    stack_blocks(block_refs, block_ref)
    half = out_ref.shape[1] // 2
    for c in (0, half):
        out_ref[:, c : c + half] = t_dot(line_ref[...], half_right(block_ref, c > 0)).astype(BF16)


def true_rows(where_ref, row, part, each, cap):
    y, z_hi = where_ref[4], where_ref[5]
    sender = over(row, each)
    inside = row - sender * each
    q = over(inside, cap)
    slot = inside - q * cap
    z = z_hi * 2 + sender % 2
    up = jnp.where(sender % 2 == 1, 1, -1)
    if part == 0:
        sources = 12
        odd = jnp.where(sender % 2 == 1, z, z - 1)
        z = jnp.where(q < 4, odd, jnp.where(q < 8, odd + 1, z + 2 * up))
        at_y = jnp.where(q < 8, q, y - q + 4 * NY)
    else:
        sources = 4
        z = z + 3 * up
        at_y = y - q + 4 * NY
    z = (z + NZ) % NZ
    source = (((z // 2) * NY + at_y % NY) * NX + sender // 2) * 2 + z % 2
    return jnp.where(q < sources, source * cap + slot, -1)


def align_kernel(dims, where_ref, saved_ref, *part_refs):
    in_group, cap = dims
    slots = saved_ref.shape[0]
    for part, ref in enumerate(part_refs):
        rows = ref.shape[0]
        true = true_rows(where_ref, iota((rows, 1), 0), part, rows // in_group, cap)
        ref[...] = dot(flag(true == iota((rows, slots), 1)), saved_ref[...]).astype(BF16)


def restore_kernel(dims, where_ref, *refs):
    in_group, cap = dims
    *part_refs, out_ref = refs
    slots = out_ref.shape[0]
    total = jnp.zeros(out_ref.shape, F32)
    for part, ref in enumerate(part_refs):
        rows = ref.shape[0]
        true = true_rows(where_ref, iota((1, rows), 1), part, rows // in_group, cap)
        total += dot(flag(true == iota((slots, rows), 0)), ref[...])
    out_ref[...] = total.astype(BF16)


def expert_kernel(x_hbm, kept_hbm, wd_hbm, wu_hbm, out_hbm, gate_hbm, x_ref, kept_ref, wd_ref, wu_ref, up_ref, out_ref, gate_ref, sems):
    hidden, features = wd_ref.shape
    rows = x_ref.shape[0]
    step, wide, tall = hidden // 3, features // 5, rows // 2 if rows > 256 else rows
    count = iter(range(sems.shape[0]))

    def copy(source, target, index):
        return pltpu.make_async_copy(source.at[index], target.at[index], sems.at[next(count)])

    tops = [pl.ds(r, tall) for r in range(0, rows, tall)]
    x = [copy(x_hbm, x_ref, t) for t in tops]
    kept = [copy(kept_hbm, kept_ref, t) for t in tops]
    down = [copy(wd_hbm, wd_ref, pl.ds(n, step)) for n in range(0, hidden, step)]
    up = [copy(wu_hbm, wu_ref, pl.ds(n, wide)) for n in range(0, features, wide)]
    for c in (x[0], down[0], kept[0], *down[1:], *x[1:], *kept[1:], *up):
        c.start()
    out = []
    for i, r in enumerate(range(0, rows, tall)):
        x[i].wait()
        for j, n in enumerate(range(0, hidden, step)):
            if i == 0:
                down[j].wait()
            grad = dot_t(x_ref[r : r + tall, :], wd_ref[n : n + step, :])
            if j == 0:
                kept[i].wait()
            act = kept_ref[r : r + tall, n : n + step].astype(F32)
            up_ref[r : r + tall, n : n + step] = (grad * act).astype(BF16)
            value = kept_ref[r : r + tall, hidden + n : hidden + n + step].astype(F32)
            gate_ref[r : r + tall, n : n + step] = (grad * value).astype(BF16)
        out.append(copy(gate_ref, gate_hbm, tops[i]))
        out[-1].start()
    for i, n in enumerate(range(0, features, wide)):
        up[i].wait()
        out_ref[:, n : n + wide] = dot_t(up_ref[...], wu_ref[n : n + wide, :]).astype(BF16)
        out.append(copy(out_ref, out_hbm, (slice(None), pl.ds(n, wide))))
        out[-1].start()
    for c in out:
        c.wait()


def device_at(z, y, x):
    return (((z // 2) % (NZ // 2) * NY + y % NY) * NX + x) * 2 + z % 2


PAIR_SETS = [
    [device_at(z % NZ, y, x) for z in (odd, odd + 1) for y in range(NY)]
    for x in range(NX)
    for odd in range(1, NZ, 2)
]


def routes_over(hops, dy, back):
    pairs = []
    for z in range(NZ):
        to = (z + (hops if (z % 2 == 1) == (hops == 3) else -hops)) % NZ
        pairs += [(device_at(z, y, x), device_at(to, y + dy, x)) for y in range(NY) for x in range(NX)]
    return [(b, a) for a, b in pairs] if back else pairs


def on_device(grad_out, route_ids, route_w, saved, w_up, w_down):
    both = ("outer", "inner")
    groups, in_group = lax.axis_size("outer"), lax.axis_size("inner")
    tok, features = grad_out.shape[1:]
    routes = route_ids.shape[2]
    slots_all = saved.shape[2]
    cap = slots_all // (groups * in_group)
    hidden = w_up.shape[3]
    group_cap = max(2, 7 * tok * ROUTE_GROUPS // (6 * groups))
    wide = SLABS * features + features // 2
    sent = wide + FIELDS
    deep = (SLABS + 1) * BLOCKS * SUB
    heights = [in_group * -(-(sources * cap) // SUB) * SUB for sources in (12, 4)]
    outer, inner = lax.axis_index("outer"), lax.axis_index("inner")
    z_hi, y, z_lo = outer // NY, outer % NY, inner % 2
    z = z_hi * 2 + z_lo
    up = 2 * z_lo - 1
    odd = (z + z_lo - 1) % NZ
    where = jnp.stack([odd, (odd + 1) % NZ, (z - 2 * up) % NZ, (z + 3 * up) % NZ, y, z_hi]).astype(I32)
    vmem, hbm = pl.BlockSpec(memory_space=pltpu.VMEM), pl.BlockSpec(memory_space=pltpu.HBM)
    smem = pl.BlockSpec(memory_space=pltpu.SMEM)

    def array(*shape):
        return jax.ShapeDtypeStruct(shape, BF16)

    def call(kernel, name, n_in, outs, mib, flops, out_specs=None, scratch=(), scalars=True):
        moved = 2 * sum(functools.reduce(lambda a, b: a * b, o.shape) for o in outs)
        return pl.pallas_call(
            kernel,
            name=name,
            in_specs=[smem] * scalars + [vmem] * n_in,
            out_specs=out_specs or [vmem] * len(outs),
            out_shape=list(outs),
            scratch_shapes=list(scratch),
            compiler_params=pltpu.CompilerParams(vmem_limit_bytes=mib * 2**20),
            cost_estimate=pl.CostEstimate(flops=flops, bytes_accessed=moved, transcendentals=0),
        )

    def near_swap(block):
        width = block.shape[1]
        moved = lax.all_to_all(block.reshape(8, SUB, width), both, 0, 0, axis_index_groups=PAIR_SETS, tiled=True)
        return moved.reshape(8 * SUB, width)

    def hop(blocks, hops, back=False):
        return [lax.ppermute(b, both, routes_over(hops, dy, back)) for dy, b in enumerate(blocks)]

    def in_groups(rows):
        moved = lax.all_to_all(rows.reshape(in_group, -1, features), "inner", 0, 0, tiled=True)
        return moved.reshape(rows.shape)

    def spread(name, blocks, rows):
        height = sum(b.shape[0] for b in blocks)
        depth = (SLABS + 1) * height
        return call(
            functools.partial(spread_kernel, (in_group, cap)), name, len(blocks),
            [array(rows, features), array(rows, depth)], 48, 2 * rows * depth * features,
            [hbm, vmem],
            [pltpu.VMEM((height, sent), BF16), pltpu.VMEM((rows, features), BF16), pltpu.SemaphoreType.DMA((2,))],
            scalars=False,
        )(*blocks)

    def gather(name, rows, hit, shapes):
        return pl.pallas_call(
            gather_kernel,
            name=name,
            in_specs=[hbm, vmem],
            out_specs=[vmem] * len(shapes),
            out_shape=[array(h, wide) for h in shapes],
            scratch_shapes=[pltpu.VMEM(rows.shape, BF16), pltpu.SemaphoreType.DMA((2,))],
            compiler_params=pltpu.CompilerParams(vmem_limit_bytes=20 * 2**20),
            cost_estimate=pl.CostEstimate(
                flops=2 * hit.shape[0] * hit.shape[1] * features, bytes_accessed=2 * rows.shape[0] * features, transcendentals=0
            ),
        )(rows, hit)

    def after(first, *values):
        *values, first = lax.optimization_barrier((*values, first))
        return first, *values

    ids, weights = (jnp.transpose(a, (2, 0, 1)) for a in (route_ids, route_w))
    shapes = [8 * SUB] + [SUB] * 8
    near, *others = call(
        functools.partial(dispatch_kernel, (groups, in_group, group_cap, cap)), "dispatch", 3,
        [array(h, sent) for h in shapes], 12, 2 * deep * tok * features,
    )(where, ids, weights, grad_out[0])
    [line] = call(
        functools.partial(lines_kernel, (groups, in_group, group_cap)), "lines", 1,
        [array(deep, tok)], 8, 4 * deep * tok * tok,
    )(where, ids)
    kept = call(
        functools.partial(align_kernel, (in_group, cap)), "align", 1, [array(h, 2 * hidden) for h in heights], 16,
        4 * sum(heights) * slots_all * hidden,
    )(where, saved[0, 0])

    near, mid, far = near_swap(near), hop(others[:4], 2), others[4:]
    near, *ready = after(near, *mid, *far)
    mid, far = ready[:4], hop(ready[4:], 3)
    rows_n, hit_n = spread("spread_near", [near, *mid], heights[0])
    rows_n = in_groups(rows_n)
    rows_f, hit_f = spread("spread_far", far, heights[1])
    rows_n, rows_f, *kept = after(rows_n, rows_f, *kept)
    rows_f = in_groups(rows_f)
    rows_n, gate_n = expert_call("expert_near", rows_n, kept[0], w_down[0, 0], w_up[0, 0])
    rows_f, rows_n = after(rows_f, rows_n)
    rows_n = in_groups(rows_n)
    rows_f, gate_f = expert_call("expert_far", rows_f, kept[1], w_down[0, 0], w_up[0, 0])
    near, *mid = gather("gather_near", rows_n, hit_n, [8 * SUB] + [SUB] * 4)
    near, rows_f, *mid = after(near, rows_f, *mid)
    mid = hop(mid, 2, True)
    rows_f = in_groups(rows_f)
    far = gather("gather_far", rows_f, hit_f, [SUB] * 4)
    near, *ready = after(near, *mid, *far)
    mid, far = ready[:4], hop(ready[4:], 3, True)
    near = near_swap(near)
    [gate_grad] = call(
        functools.partial(restore_kernel, (in_group, cap)), "restore", 2, [array(slots_all, hidden)], 12,
        2 * sum(heights) * slots_all * hidden,
    )(where, gate_n, gate_f)
    gate_grad, line = after(gate_grad, line)
    [token_grad] = call(
        combine_kernel, "combine", 10, [array(tok, features)], 12, 2 * deep * tok * features,
        scratch=[pltpu.VMEM((BLOCKS * SUB, wide), BF16)], scalars=False,
    )(near, *mid, *far, line)
    count = lax.axis_size("section")
    received = lax.ppermute(token_grad, "section", [((i + 1) % count, i) for i in range(count)])
    return (received[None], gate_grad[None, None])


def expert_call(name, rows, kept, w_down, w_up):
    hidden, features = w_down.shape
    height = rows.shape[0]
    hbm = pl.BlockSpec(memory_space=pltpu.HBM)
    return pl.pallas_call(
        expert_kernel,
        name=name,
        in_specs=[hbm] * 4,
        out_specs=[hbm] * 2,
        out_shape=[jax.ShapeDtypeStruct((height, features), BF16), jax.ShapeDtypeStruct((height, hidden), BF16)],
        scratch_shapes=[
            pltpu.VMEM((height, features), BF16),
            pltpu.VMEM((height, 2 * hidden), BF16),
            pltpu.VMEM((hidden, features), BF16),
            pltpu.VMEM((features, hidden), BF16),
            pltpu.VMEM((height, hidden), BF16),
            pltpu.VMEM((height, features), BF16),
            pltpu.VMEM((height, hidden), BF16),
            pltpu.SemaphoreType.DMA((19,)),
        ],
        compiler_params=pltpu.CompilerParams(vmem_limit_bytes=56 * 2**20),
        cost_estimate=pl.CostEstimate(
            flops=4 * height * features * hidden, bytes_accessed=4 * (height + hidden) * features, transcendentals=0
        ),
    )(rows, kept, w_down, w_up)


def solution(mesh):
    return jax.shard_map(
        on_device,
        mesh=mesh,
        in_specs=(
            P("section", ("outer", "inner"), None),
            P("section", ("outer", "inner"), None),
            P("section", ("outer", "inner"), None),
            P("section", ("outer", "inner"), None, None),
            P("section", ("outer", "inner"), None, None),
            P("section", ("outer", "inner"), None, None),
        ),
        out_specs=(
            P("section", ("outer", "inner"), None),
            P("section", ("outer", "inner"), None, None),
        ),
        check_vma=False,
    )
```

```python
import functools
import jax
import jax.numpy as jnp
from jax import lax
from jax.experimental import pallas as pl
from jax.experimental.pallas import tpu as pltpu
from jax.sharding import PartitionSpec as P

NZ, NY, NX = 8, 4, 4
ROUTE_GROUPS = 3
SUB = 8
SLABS = 3
FIELDS = 128
BLOCKS = 16
F32 = jnp.float32
BF16 = jnp.bfloat16
I32 = jnp.int32


def iota(shape, dim):
    return lax.broadcasted_iota(I32, shape, dim)


def dot(a, b):
    return lax.dot_general(a, b, (((1,), (0,)), ((), ())), preferred_element_type=F32)


def dot_t(a, b):
    return lax.dot_general(a, b, (((1,), (1,)), ((), ())), preferred_element_type=F32)


def t_dot(a, b):
    return lax.dot_general(a, b, (((0,), (0,)), ((), ())), preferred_element_type=F32)


def flag(mask, kind=BF16):
    return jnp.where(mask, 1.0, 0.0).astype(kind)


def over(value, divisor):
    return jnp.floor((value.astype(F32) + 0.5) * (1.0 / divisor)).astype(I32)


def top_bits(value):
    wide = value * 65537.0
    return wide - (wide - value)


def block_group(where_ref, block):
    odd, even, mid, far, y = (where_ref[i] for i in range(5))
    z = jnp.where(block < 4, odd, jnp.where(block < 8, even, jnp.where(block < 12, mid, far)))
    return (z // 2) * NY + jnp.where(block < 8, block % NY, (block + y) % NY)


def slots_in_group(member, group_cap):
    tok = member.shape[1]
    before = flag(iota((tok, tok), 0) < iota((tok, tok), 1))
    rank = dot(member.astype(BF16), before)
    return jnp.where((member > 0) & (rank < group_cap), rank, -1.0)


def token_lines(where_ref, group_slot):
    groups, tok = group_slot.shape
    rows = (SLABS + 1) * BLOCKS * SUB
    r = iota((rows, groups), 0)
    chosen = flag(block_group(where_ref, (r // SUB) % BLOCKS) == iota((rows, groups), 1))
    r = iota((rows, tok), 0)
    slab, sub = r // (BLOCKS * SUB), r % SUB
    slot = jnp.where(slab == SLABS, SLABS * SUB + sub % 4, slab * SUB + sub)
    return flag(dot(chosen, group_slot.astype(BF16)) == slot.astype(F32))


def half_rows(value, second):
    sub = iota(value.shape, 0) % SUB
    return jnp.where(sub >= 4 if second else sub < 4, value, jnp.zeros_like(value))


def half_right(block_ref, second):
    features = block_ref.shape[1] // (2 * SLABS + 1) // FIELDS * FIELDS * 2
    half, tail = features // 2, SLABS * features
    c = half if second else 0
    last = half_rows(block_ref[:, tail : tail + half].astype(F32), second).astype(BF16)
    return jnp.concatenate([*(block_ref[:, n * features + c : n * features + c + half] for n in range(SLABS)), last], axis=0)


def lines_kernel(dims, where_ref, ids_ref, line_ref):
    groups, in_group, group_cap = dims
    routes, _, tok = ids_ref.shape
    member = jnp.zeros((groups, tok), F32)
    for k in range(0, routes, routes // ROUTE_GROUPS):
        member += flag(ids_ref[k] // in_group == iota((groups, tok), 0), F32)
    line_ref[...] = token_lines(where_ref, slots_in_group(member, group_cap))


def send_columns(block_ref, block_hbm, sems, copies, start, width):
    columns = (slice(None), pl.ds(start, width))
    copies.append(pltpu.make_async_copy(block_ref.at[columns], block_hbm.at[columns], sems.at[len(copies)]))
    copies[-1].start()


def put_blocks(block_refs, value, start):
    row = 0
    for ref in block_refs:
        ref[:, start : start + value.shape[1]] = value[row : row + ref.shape[0]].astype(BF16)
        row += ref.shape[0]


def stack_blocks(block_refs, stacked_ref):
    width, row, first = stacked_ref.shape[1], 0, None
    for ref in block_refs:
        if ref.shape[0] > SUB:
            stacked_ref[row : row + ref.shape[0], :] = ref[:, :width]
            row += ref.shape[0]
        elif first is None:
            first = ref
        else:
            pair = jnp.concatenate([first[:, :width].astype(F32), ref[:, :width].astype(F32)], axis=0)
            stacked_ref[row : row + 2 * SUB, :] = pair.astype(BF16)
            row, first = row + 2 * SUB, None


def dispatch_kernel(dims, where_ref, ids_ref, w_ref, g_ref, near_hbm, *refs):
    *block_refs, near_ref, sems = refs
    block_refs, copies = [near_ref, *block_refs], []
    groups, in_group, group_cap, cap = dims
    routes, _, tok = ids_ref.shape
    features, experts = g_ref.shape[1], groups * in_group
    half, per = features // 2, routes // ROUTE_GROUPS
    e, group = iota((experts, tok), 0), iota((groups, tok), 0)
    before = flag(iota((tok, tok), 0) < iota((tok, tok), 1))
    ids = [ids_ref[k] for k in range(routes)]
    named = jnp.zeros((experts, tok), F32)
    mine = jnp.zeros((experts, tok), F32)
    member = jnp.zeros((groups, tok), F32)
    for k in range(routes):
        named += flag(ids[k] == e, F32)
        if k % per == 0:
            mine += flag(ids[k] // in_group == e // in_group, F32)
            member += flag(ids[k] // in_group == group, F32)
    admitted = (named > 0) & (dot(mine.astype(BF16), before) < group_cap)
    slot_rank = dot(flag(admitted), before)
    rank = jnp.where(admitted & (slot_rank < cap), slot_rank, -1.0)
    group_slot = slots_in_group(member, group_cap)
    fields = [jnp.zeros((groups, tok), F32) for _ in range(SUB)]
    for k in range(routes):
        own = jnp.sum(jnp.where(ids[k] == e, rank, 0.0), axis=0, keepdims=True)
        place = jnp.where(own >= 0, (ids[k] % in_group).astype(F32) * cap + own + 1.0, 0.0)
        weight = w_ref[k]
        first = top_bits(weight)
        second = top_bits(weight - first)
        third = (weight - first) - second
        at = ids[k] // in_group == group
        for f, value in ((k % per, place), *((per + 3 * (k % per) + i, v) for i, v in enumerate((first, second, third)))):
            fields[f] += jnp.where(at, value, 0.0)
    stacked = jnp.concatenate([f.astype(BF16) for f in fields], axis=0)
    line = token_lines(where_ref, group_slot)
    rows, part = line.shape[0], groups * SUB
    r, c = iota((part, part), 0), iota((part, part), 1)
    choose = flag((block_group(where_ref, r // SUB) == c % groups) & (r % SUB == c // groups))
    by_block = dot(choose, stacked).astype(BF16)
    by_slot = dot_t(by_block, line)
    r, c = iota((part, rows), 0), iota((part, rows), 1)
    by_slot = jnp.where((c // SUB) % groups == r // SUB, by_slot, 0.0).astype(BF16)
    r, c = iota((rows, FIELDS), 0), iota((rows, FIELDS), 1)
    fold = flag(c == (r // part) * SUB + r % SUB)
    block_fields = dot(by_slot, fold)

    def put(value, start, width):
        put_blocks(block_refs, value, start)
        send_columns(near_ref, near_hbm, sems, copies, start, width)

    for n in range(SLABS):
        for c in (0, half):
            put(dot(line[n * part : (n + 1) * part], g_ref[:, c : c + half]), n * features + c, half)
    line = line[SLABS * part :]
    put(
        half_rows(dot(line, g_ref[:, :half]), False) + half_rows(dot(line, g_ref[:, half:]), True),
        SLABS * features, half,
    )
    put(block_fields, SLABS * features + half, FIELDS)
    for copy in copies:
        copy.wait()


def spread_kernel(dims, *refs):
    *block_refs, out_hbm, hit_ref, block_ref, out_ref, sems = refs
    stack_blocks(block_refs, block_ref)
    in_group, cap = dims
    height, features = block_ref.shape[0], out_ref.shape[1]
    sources = height // SUB
    half, tail = features // 2, SLABS * features

    deep = (SLABS + 1) * height
    l, c = iota((FIELDS, deep), 0), iota((FIELDS, deep), 1)
    unfold = flag((l == (c // height) * SUB + c % SUB) & (l < (SLABS + 1) * SUB))
    wide = dot(block_ref[:, tail + half :], unfold)
    r, c = iota((height, deep), 0), iota((height, deep), 1)
    wide = jnp.where(r // SUB == (c // SUB) % sources, wide, 0.0)
    fields = wide[:SUB]
    for q in range(1, sources):
        fields += wide[q * SUB : (q + 1) * SUB]
    places = [fields[k : k + 1].astype(I32) for k in range(2)]
    weights = [(fields[2 + 3 * k : 3 + 3 * k] + fields[3 + 3 * k : 4 + 3 * k]) + fields[4 + 3 * k : 5 + 3 * k] for k in range(2)]
    rows = out_ref.shape[0]
    s = iota((rows, 1), 0)
    each = rows // in_group
    expert = over(s, each)
    inside = s - expert * each
    source = over(inside, cap)
    key = source * 64 + expert * cap + (inside - source * cap) + 1
    key = jnp.where(source < sources, key, -2)
    c = iota((1, deep), 1)
    base = ((c // SUB) % sources) * 64
    hits = [key == jnp.where(place > 0, base + place, -1) for place in places]
    once = iota((1, deep), 1)
    once = (once < SLABS * height) | (once % SUB < 4)
    hit_ref[...] = flag(hits[0] | hits[1])
    scale = jnp.where(hits[0], jnp.where(once, weights[0], 0.0), 0.0)
    scale += jnp.where(hits[1], jnp.where(once, weights[1], 0.0), 0.0)
    scale = jnp.sum(scale, axis=1, keepdims=True)
    copies = []
    for c in (0, half):
        out_ref[:, c : c + half] = (dot(hit_ref[...], half_right(block_ref, c > 0)) * scale).astype(BF16)
        copies.append(
            pltpu.make_async_copy(out_ref.at[:, pl.ds(c, half)], out_hbm.at[:, pl.ds(c, half)], sems.at[c // half])
        )
        copies[-1].start()
    for copy in copies:
        copy.wait()


def gather_kernel(rows_hbm, hit_ref, *refs):
    *block_refs, rows_ref, sems, out_sems = refs
    features, height = rows_ref.shape[1], hit_ref.shape[1] // (SLABS + 1)
    half = features // 2
    tall = block_refs[0].shape[0] > SUB
    if tall:
        block_hbm, *block_refs, block_ref = block_refs
        block_refs = [block_ref, *block_refs]
    outs = []

    def put(value, start):
        put_blocks(block_refs, value, start)
        if tall:
            send_columns(block_ref, block_hbm, out_sems, outs, start, half)

    copies = [
        pltpu.make_async_copy(rows_hbm.at[:, pl.ds(c, half)], rows_ref.at[:, pl.ds(c, half)], sems.at[c // half])
        for c in (0, half)
    ]
    for copy in copies:
        copy.start()
    tail = jnp.zeros((height, half), F32)
    for copy, c in zip(copies, (0, half), strict=True):
        copy.wait()
        got = t_dot(hit_ref[...], rows_ref[:, c : c + half])
        for n in range(SLABS):
            put(got[n * height : (n + 1) * height], n * features + c)
        tail += half_rows(got[SLABS * height :], c > 0)
    put(tail, SLABS * features)
    for copy in outs:
        copy.wait()


def combine_kernel(*refs):
    *block_refs, line_ref, out_ref, block_ref = refs
    stack_blocks(block_refs, block_ref)
    half = out_ref.shape[1] // 2
    for c in (0, half):
        out_ref[:, c : c + half] = t_dot(line_ref[...], half_right(block_ref, c > 0)).astype(BF16)


def true_rows(where_ref, row, part, each, cap):
    y, z_hi = where_ref[4], where_ref[5]
    sender = over(row, each)
    inside = row - sender * each
    q = over(inside, cap)
    slot = inside - q * cap
    z = z_hi * 2 + sender % 2
    up = jnp.where(sender % 2 == 1, 1, -1)
    if part == 0:
        sources = 12
        odd = jnp.where(sender % 2 == 1, z, z - 1)
        z = jnp.where(q < 4, odd, jnp.where(q < 8, odd + 1, z + 2 * up))
        at_y = jnp.where(q < 8, q, y - q + 4 * NY)
    else:
        sources = 4
        z = z + 3 * up
        at_y = y - q + 4 * NY
    z = (z + NZ) % NZ
    source = (((z // 2) * NY + at_y % NY) * NX + sender // 2) * 2 + z % 2
    return jnp.where(q < sources, source * cap + slot, -1)


def align_kernel(dims, where_ref, saved_ref, *part_refs):
    in_group, cap = dims
    slots = saved_ref.shape[0]
    for part, ref in enumerate(part_refs):
        rows = ref.shape[0]
        true = true_rows(where_ref, iota((rows, 1), 0), part, rows // in_group, cap)
        ref[...] = dot(flag(true == iota((rows, slots), 1)), saved_ref[...]).astype(BF16)


def restore_kernel(dims, where_ref, *refs):
    in_group, cap = dims
    *part_refs, out_ref = refs
    slots = out_ref.shape[0]
    total = jnp.zeros(out_ref.shape, F32)
    for part, ref in enumerate(part_refs):
        rows = ref.shape[0]
        true = true_rows(where_ref, iota((1, rows), 1), part, rows // in_group, cap)
        total += dot(flag(true == iota((slots, rows), 0)), ref[...])
    out_ref[...] = total.astype(BF16)


def expert_kernel(x_hbm, kept_hbm, wd_hbm, wu_hbm, out_hbm, gate_hbm, x_ref, kept_ref, wd_ref, wu_ref, up_ref, out_ref, gate_ref, sems):
    hidden, features = wd_ref.shape
    rows = x_ref.shape[0]
    step, wide, tall = hidden // 3, features // 5, rows // 2 if rows > 256 else rows
    count = iter(range(sems.shape[0]))

    def copy(source, target, index):
        return pltpu.make_async_copy(source.at[index], target.at[index], sems.at[next(count)])

    tops = [pl.ds(r, tall) for r in range(0, rows, tall)]
    x = [copy(x_hbm, x_ref, t) for t in tops]
    kept = [copy(kept_hbm, kept_ref, t) for t in tops]
    down = [copy(wd_hbm, wd_ref, pl.ds(n, step)) for n in range(0, hidden, step)]
    up = [copy(wu_hbm, wu_ref, pl.ds(n, wide)) for n in range(0, features, wide)]
    for c in (x[0], down[0], kept[0], *down[1:], *x[1:], *kept[1:], *up):
        c.start()
    out = []
    for i, r in enumerate(range(0, rows, tall)):
        x[i].wait()
        for j, n in enumerate(range(0, hidden, step)):
            if i == 0:
                down[j].wait()
            grad = dot_t(x_ref[r : r + tall, :], wd_ref[n : n + step, :])
            if j == 0:
                kept[i].wait()
            act = kept_ref[r : r + tall, n : n + step].astype(F32)
            up_ref[r : r + tall, n : n + step] = (grad * act).astype(BF16)
            value = kept_ref[r : r + tall, hidden + n : hidden + n + step].astype(F32)
            gate_ref[r : r + tall, n : n + step] = (grad * value).astype(BF16)
        out.append(copy(gate_ref, gate_hbm, tops[i]))
        out[-1].start()
    for i, n in enumerate(range(0, features, wide)):
        up[i].wait()
        out_ref[:, n : n + wide] = dot_t(up_ref[...], wu_ref[n : n + wide, :]).astype(BF16)
        out.append(copy(out_ref, out_hbm, (slice(None), pl.ds(n, wide))))
        out[-1].start()
    for c in out:
        c.wait()


def device_at(z, y, x):
    return (((z // 2) % (NZ // 2) * NY + y % NY) * NX + x) * 2 + z % 2


PAIR_SETS = [
    [device_at(z % NZ, y, x) for z in (odd, odd + 1) for y in range(NY)]
    for x in range(NX)
    for odd in range(1, NZ, 2)
]


def routes_over(hops, dy, back):
    pairs = []
    for z in range(NZ):
        to = (z + (hops if (z % 2 == 1) == (hops == 3) else -hops)) % NZ
        pairs += [(device_at(z, y, x), device_at(to, y + dy, x)) for y in range(NY) for x in range(NX)]
    return [(b, a) for a, b in pairs] if back else pairs


def on_device(grad_out, route_ids, route_w, saved, w_up, w_down):
    both = ("outer", "inner")
    groups, in_group = lax.axis_size("outer"), lax.axis_size("inner")
    tok, features = grad_out.shape[1:]
    routes = route_ids.shape[2]
    slots_all = saved.shape[2]
    cap = slots_all // (groups * in_group)
    hidden = w_up.shape[3]
    group_cap = max(2, 7 * tok * ROUTE_GROUPS // (6 * groups))
    wide = SLABS * features + features // 2
    sent = wide + FIELDS
    deep = (SLABS + 1) * BLOCKS * SUB
    heights = [in_group * -(-(sources * cap) // SUB) * SUB for sources in (12, 4)]
    outer, inner = lax.axis_index("outer"), lax.axis_index("inner")
    z_hi, y, z_lo = outer // NY, outer % NY, inner % 2
    z = z_hi * 2 + z_lo
    up = 2 * z_lo - 1
    odd = (z + z_lo - 1) % NZ
    where = jnp.stack([odd, (odd + 1) % NZ, (z - 2 * up) % NZ, (z + 3 * up) % NZ, y, z_hi]).astype(I32)
    vmem, hbm = pl.BlockSpec(memory_space=pltpu.VMEM), pl.BlockSpec(memory_space=pltpu.HBM)
    smem = pl.BlockSpec(memory_space=pltpu.SMEM)

    def array(*shape):
        return jax.ShapeDtypeStruct(shape, BF16)

    def call(kernel, name, n_in, outs, mib, flops, out_specs=None, scratch=(), scalars=True):
        moved = 2 * sum(functools.reduce(lambda a, b: a * b, o.shape) for o in outs)
        return pl.pallas_call(
            kernel,
            name=name,
            in_specs=[smem] * scalars + [vmem] * n_in,
            out_specs=out_specs or [vmem] * len(outs),
            out_shape=list(outs),
            scratch_shapes=list(scratch),
            compiler_params=pltpu.CompilerParams(vmem_limit_bytes=mib * 2**20),
            cost_estimate=pl.CostEstimate(flops=flops, bytes_accessed=moved, transcendentals=0),
        )

    def near_swap(block):
        width = block.shape[1]
        moved = lax.all_to_all(block.reshape(8, SUB, width), both, 0, 0, axis_index_groups=PAIR_SETS, tiled=True)
        return moved.reshape(8 * SUB, width)

    def hop(blocks, hops, back=False):
        return [lax.ppermute(b, both, routes_over(hops, dy, back)) for dy, b in enumerate(blocks)]

    def in_groups(rows):
        moved = lax.all_to_all(rows.reshape(in_group, -1, features), "inner", 0, 0, tiled=True)
        return moved.reshape(rows.shape)

    def spread(name, blocks, rows):
        height = sum(b.shape[0] for b in blocks)
        depth = (SLABS + 1) * height
        return call(
            functools.partial(spread_kernel, (in_group, cap)), name, len(blocks),
            [array(rows, features), array(rows, depth)], 48, 2 * rows * depth * features,
            [hbm, vmem],
            [pltpu.VMEM((height, sent), BF16), pltpu.VMEM((rows, features), BF16), pltpu.SemaphoreType.DMA((2,))],
            scalars=False,
        )(*blocks)

    def gather(name, rows, hit, shapes):
        return pl.pallas_call(
            gather_kernel,
            name=name,
            in_specs=[hbm, vmem],
            out_specs=[hbm if h > SUB else vmem for h in shapes],
            out_shape=[array(h, wide) for h in shapes],
            scratch_shapes=[
                *(pltpu.VMEM((h, wide), BF16) for h in shapes if h > SUB),
                pltpu.VMEM(rows.shape, BF16),
                pltpu.SemaphoreType.DMA((2,)),
                pltpu.SemaphoreType.DMA((2 * SLABS + 1,)),
            ],
            compiler_params=pltpu.CompilerParams(vmem_limit_bytes=20 * 2**20),
            cost_estimate=pl.CostEstimate(
                flops=2 * hit.shape[0] * hit.shape[1] * features, bytes_accessed=2 * rows.shape[0] * features, transcendentals=0
            ),
        )(rows, hit)

    def after(first, *values):
        *values, first = lax.optimization_barrier((*values, first))
        return first, *values

    ids, weights = (jnp.transpose(a, (2, 0, 1)) for a in (route_ids, route_w))
    shapes = [8 * SUB] + [SUB] * 8
    near, *others = call(
        functools.partial(dispatch_kernel, (groups, in_group, group_cap, cap)), "dispatch", 3,
        [array(h, sent) for h in shapes], 12, 2 * deep * tok * features, [hbm] + [vmem] * 8,
        [pltpu.VMEM((8 * SUB, sent), BF16), pltpu.SemaphoreType.DMA((2 * SLABS + 2,))],
    )(where, ids, weights, grad_out[0])
    [line] = call(
        functools.partial(lines_kernel, (groups, in_group, group_cap)), "lines", 1,
        [array(deep, tok)], 8, 4 * deep * tok * tok,
    )(where, ids)
    kept = call(
        functools.partial(align_kernel, (in_group, cap)), "align", 1, [array(h, 2 * hidden) for h in heights], 16,
        4 * sum(heights) * slots_all * hidden,
    )(where, saved[0, 0])

    near, mid, far = near_swap(near), hop(others[:4], 2), others[4:]
    near, *ready = after(near, *mid, *far)
    mid, far = ready[:4], hop(ready[4:], 3)
    rows_n, hit_n = spread("spread_near", [near, *mid], heights[0])
    rows_n = in_groups(rows_n)
    rows_f, hit_f = spread("spread_far", far, heights[1])
    rows_n, rows_f = after(rows_n, rows_f)
    rows_f = in_groups(rows_f)
    rows_n, gate_n = expert_call("expert_near", rows_n, kept[0], w_down[0, 0], w_up[0, 0])
    rows_f, gate_f = expert_call("expert_far", rows_f, kept[1], w_down[0, 0], w_up[0, 0])
    rows_f = in_groups(rows_f)
    far = gather("gather_far", rows_f, hit_f, [SUB] * 4)
    rows_n, *far = after(rows_n, *far)
    far = hop(far, 3, True)
    rows_n = in_groups(rows_n)
    rows_n, *far = after(rows_n, *far)
    [gate_grad] = call(
        functools.partial(restore_kernel, (in_group, cap)), "restore", 2, [array(slots_all, hidden)], 12,
        2 * sum(heights) * slots_all * hidden,
    )(where, gate_n, gate_f)
    near, *mid = gather("gather_near", rows_n, hit_n, [8 * SUB] + [SUB] * 4)
    near, mid = near_swap(near), hop(mid, 2, True)
    gate_grad, line = after(gate_grad, line)
    [token_grad] = call(
        combine_kernel, "combine", 10, [array(tok, features)], 12, 2 * deep * tok * features,
        scratch=[pltpu.VMEM((BLOCKS * SUB, wide), BF16)], scalars=False,
    )(near, *mid, *far, line)
    count = lax.axis_size("section")
    received = lax.ppermute(token_grad, "section", [((i + 1) % count, i) for i in range(count)])
    return (received[None], gate_grad[None, None])


def expert_call(name, rows, kept, w_down, w_up):
    hidden, features = w_down.shape
    height = rows.shape[0]
    hbm = pl.BlockSpec(memory_space=pltpu.HBM)
    return pl.pallas_call(
        expert_kernel,
        name=name,
        in_specs=[hbm] * 4,
        out_specs=[hbm] * 2,
        out_shape=[jax.ShapeDtypeStruct((height, features), BF16), jax.ShapeDtypeStruct((height, hidden), BF16)],
        scratch_shapes=[
            pltpu.VMEM((height, features), BF16),
            pltpu.VMEM((height, 2 * hidden), BF16),
            pltpu.VMEM((hidden, features), BF16),
            pltpu.VMEM((features, hidden), BF16),
            pltpu.VMEM((height, hidden), BF16),
            pltpu.VMEM((height, features), BF16),
            pltpu.VMEM((height, hidden), BF16),
            pltpu.SemaphoreType.DMA((19,)),
        ],
        compiler_params=pltpu.CompilerParams(vmem_limit_bytes=56 * 2**20),
        cost_estimate=pl.CostEstimate(
            flops=4 * height * features * hidden, bytes_accessed=4 * (height + hidden) * features, transcendentals=0
        ),
    )(rows, kept, w_down, w_up)


def solution(mesh):
    return jax.shard_map(
        on_device,
        mesh=mesh,
        in_specs=(
            P("section", ("outer", "inner"), None),
            P("section", ("outer", "inner"), None),
            P("section", ("outer", "inner"), None),
            P("section", ("outer", "inner"), None, None),
            P("section", ("outer", "inner"), None, None),
            P("section", ("outer", "inner"), None, None),
        ),
        out_specs=(
            P("section", ("outer", "inner"), None),
            P("section", ("outer", "inner"), None, None),
        ),
        check_vma=False,
    )
```

```python
import functools
import jax
import jax.numpy as jnp
from jax import lax
from jax.experimental import pallas as pl
from jax.experimental.pallas import tpu as pltpu
from jax.sharding import PartitionSpec as P

NZ, NY, NX = 8, 4, 4
ROUTE_GROUPS = 3
SUB = 8
SLABS = 3
FIELDS = 128
BLOCKS = 16
F32 = jnp.float32
BF16 = jnp.bfloat16
I32 = jnp.int32


def iota(shape, dim):
    return lax.broadcasted_iota(I32, shape, dim)


def dot(a, b):
    return lax.dot_general(a, b, (((1,), (0,)), ((), ())), preferred_element_type=F32)


def dot_t(a, b):
    return lax.dot_general(a, b, (((1,), (1,)), ((), ())), preferred_element_type=F32)


def t_dot(a, b):
    return lax.dot_general(a, b, (((0,), (0,)), ((), ())), preferred_element_type=F32)


def flag(mask, kind=BF16):
    return jnp.where(mask, 1.0, 0.0).astype(kind)


def over(value, divisor):
    return jnp.floor((value.astype(F32) + 0.5) * (1.0 / divisor)).astype(I32)


def top_bits(value):
    wide = value * 65537.0
    return wide - (wide - value)


def block_group(where_ref, block):
    odd, even, mid, far, y = (where_ref[i] for i in range(5))
    z = jnp.where(block < 4, odd, jnp.where(block < 8, even, jnp.where(block < 12, mid, far)))
    return (z // 2) * NY + jnp.where(block < 8, block % NY, (block + y) % NY)


def slots_in_group(member, group_cap):
    tok = member.shape[1]
    before = flag(iota((tok, tok), 0) < iota((tok, tok), 1))
    rank = dot(member.astype(BF16), before)
    return jnp.where((member > 0) & (rank < group_cap), rank, -1.0)


def token_lines(where_ref, group_slot):
    groups, tok = group_slot.shape
    rows = (SLABS + 1) * BLOCKS * SUB
    r = iota((rows, groups), 0)
    chosen = flag(block_group(where_ref, (r // SUB) % BLOCKS) == iota((rows, groups), 1))
    r = iota((rows, tok), 0)
    slab, sub = r // (BLOCKS * SUB), r % SUB
    slot = jnp.where(slab == SLABS, SLABS * SUB + sub % 4, slab * SUB + sub)
    return flag(dot(chosen, group_slot.astype(BF16)) == slot.astype(F32))


def half_rows(value, second):
    sub = iota(value.shape, 0) % SUB
    return jnp.where(sub >= 4 if second else sub < 4, value, jnp.zeros_like(value))


def half_right(block_ref, second):
    features = block_ref.shape[1] // (2 * SLABS + 1) // FIELDS * FIELDS * 2
    half, tail = features // 2, SLABS * features
    c = half if second else 0
    last = half_rows(block_ref[:, tail : tail + half].astype(F32), second).astype(BF16)
    return jnp.concatenate([*(block_ref[:, n * features + c : n * features + c + half] for n in range(SLABS)), last], axis=0)


def lines_kernel(dims, where_ref, ids_ref, line_ref):
    groups, in_group, group_cap = dims
    routes, _, tok = ids_ref.shape
    member = jnp.zeros((groups, tok), F32)
    for k in range(0, routes, routes // ROUTE_GROUPS):
        member += flag(ids_ref[k] // in_group == iota((groups, tok), 0), F32)
    line_ref[...] = token_lines(where_ref, slots_in_group(member, group_cap))


def send_columns(block_ref, block_hbm, sems, copies, start, width):
    columns = (slice(None), pl.ds(start, width))
    copies.append(pltpu.make_async_copy(block_ref.at[columns], block_hbm.at[columns], sems.at[len(copies)]))
    copies[-1].start()


def put_blocks(block_refs, value, start):
    row = 0
    for ref in block_refs:
        ref[:, start : start + value.shape[1]] = value[row : row + ref.shape[0]].astype(BF16)
        row += ref.shape[0]


def stack_blocks(block_refs, stacked_ref):
    width, row, first = stacked_ref.shape[1], 0, None
    for ref in block_refs:
        if ref.shape[0] > SUB:
            stacked_ref[row : row + ref.shape[0], :] = ref[:, :width]
            row += ref.shape[0]
        elif first is None:
            first = ref
        else:
            pair = jnp.concatenate([first[:, :width].astype(F32), ref[:, :width].astype(F32)], axis=0)
            stacked_ref[row : row + 2 * SUB, :] = pair.astype(BF16)
            row, first = row + 2 * SUB, None


def dispatch_kernel(dims, where_ref, ids_ref, w_ref, g_ref, near_hbm, *refs):
    *block_refs, near_ref, sems = refs
    block_refs, copies = [near_ref, *block_refs], []
    groups, in_group, group_cap, cap = dims
    routes, _, tok = ids_ref.shape
    features, experts = g_ref.shape[1], groups * in_group
    half, per = features // 2, routes // ROUTE_GROUPS
    e, group = iota((experts, tok), 0), iota((groups, tok), 0)
    before = flag(iota((tok, tok), 0) < iota((tok, tok), 1))
    ids = [ids_ref[k] for k in range(routes)]
    named = jnp.zeros((experts, tok), F32)
    mine = jnp.zeros((experts, tok), F32)
    member = jnp.zeros((groups, tok), F32)
    for k in range(routes):
        named += flag(ids[k] == e, F32)
        if k % per == 0:
            mine += flag(ids[k] // in_group == e // in_group, F32)
            member += flag(ids[k] // in_group == group, F32)
    admitted = (named > 0) & (dot(mine.astype(BF16), before) < group_cap)
    slot_rank = dot(flag(admitted), before)
    rank = jnp.where(admitted & (slot_rank < cap), slot_rank, -1.0)
    group_slot = slots_in_group(member, group_cap)
    fields = [jnp.zeros((groups, tok), F32) for _ in range(SUB)]
    for k in range(routes):
        own = jnp.sum(jnp.where(ids[k] == e, rank, 0.0), axis=0, keepdims=True)
        place = jnp.where(own >= 0, (ids[k] % in_group).astype(F32) * cap + own + 1.0, 0.0)
        weight = w_ref[k]
        first = top_bits(weight)
        second = top_bits(weight - first)
        third = (weight - first) - second
        at = ids[k] // in_group == group
        for f, value in ((k % per, place), *((per + 3 * (k % per) + i, v) for i, v in enumerate((first, second, third)))):
            fields[f] += jnp.where(at, value, 0.0)
    stacked = jnp.concatenate([f.astype(BF16) for f in fields], axis=0)
    line = token_lines(where_ref, group_slot)
    rows, part = line.shape[0], groups * SUB
    r, c = iota((part, part), 0), iota((part, part), 1)
    choose = flag((block_group(where_ref, r // SUB) == c % groups) & (r % SUB == c // groups))
    by_block = dot(choose, stacked).astype(BF16)
    by_slot = dot_t(by_block, line)
    r, c = iota((part, rows), 0), iota((part, rows), 1)
    by_slot = jnp.where((c // SUB) % groups == r // SUB, by_slot, 0.0).astype(BF16)
    r, c = iota((rows, FIELDS), 0), iota((rows, FIELDS), 1)
    fold = flag(c == (r // part) * SUB + r % SUB)
    block_fields = dot(by_slot, fold)

    def put(value, start, width):
        put_blocks(block_refs, value, start)
        send_columns(near_ref, near_hbm, sems, copies, start, width)

    for n in range(SLABS):
        for c in (0, half):
            put(dot(line[n * part : (n + 1) * part], g_ref[:, c : c + half]), n * features + c, half)
    line = line[SLABS * part :]
    put(
        half_rows(dot(line, g_ref[:, :half]), False) + half_rows(dot(line, g_ref[:, half:]), True),
        SLABS * features, half,
    )
    put(block_fields, SLABS * features + half, FIELDS)
    for copy in copies:
        copy.wait()


def spread_kernel(dims, *refs):
    *block_refs, out_hbm, hit_ref, block_ref, out_ref, sems = refs
    stack_blocks(block_refs, block_ref)
    in_group, cap = dims
    height, features = block_ref.shape[0], out_ref.shape[1]
    sources = height // SUB
    half, tail = features // 2, SLABS * features

    deep = (SLABS + 1) * height
    l, c = iota((FIELDS, deep), 0), iota((FIELDS, deep), 1)
    unfold = flag((l == (c // height) * SUB + c % SUB) & (l < (SLABS + 1) * SUB))
    wide = dot(block_ref[:, tail + half :], unfold)
    r, c = iota((height, deep), 0), iota((height, deep), 1)
    wide = jnp.where(r // SUB == (c // SUB) % sources, wide, 0.0)
    fields = wide[:SUB]
    for q in range(1, sources):
        fields += wide[q * SUB : (q + 1) * SUB]
    places = [fields[k : k + 1].astype(I32) for k in range(2)]
    weights = [(fields[2 + 3 * k : 3 + 3 * k] + fields[3 + 3 * k : 4 + 3 * k]) + fields[4 + 3 * k : 5 + 3 * k] for k in range(2)]
    rows = out_ref.shape[0]
    s = iota((rows, 1), 0)
    each = rows // in_group
    expert = over(s, each)
    inside = s - expert * each
    source = over(inside, cap)
    key = source * 64 + expert * cap + (inside - source * cap) + 1
    key = jnp.where(source < sources, key, -2)
    c = iota((1, deep), 1)
    base = ((c // SUB) % sources) * 64
    hits = [key == jnp.where(place > 0, base + place, -1) for place in places]
    once = iota((1, deep), 1)
    once = (once < SLABS * height) | (once % SUB < 4)
    hit_ref[...] = flag(hits[0] | hits[1])
    scale = jnp.where(hits[0], jnp.where(once, weights[0], 0.0), 0.0)
    scale += jnp.where(hits[1], jnp.where(once, weights[1], 0.0), 0.0)
    scale = jnp.sum(scale, axis=1, keepdims=True)
    copies = []
    for c in (0, half):
        out_ref[:, c : c + half] = (dot(hit_ref[...], half_right(block_ref, c > 0)) * scale).astype(BF16)
        copies.append(
            pltpu.make_async_copy(out_ref.at[:, pl.ds(c, half)], out_hbm.at[:, pl.ds(c, half)], sems.at[c // half])
        )
        copies[-1].start()
    for copy in copies:
        copy.wait()


def gather_kernel(rows_hbm, hit_ref, *refs):
    *block_refs, rows_ref, sems, out_sems = refs
    features, height = rows_ref.shape[1], hit_ref.shape[1] // (SLABS + 1)
    half = features // 2
    tall = block_refs[0].shape[0] > SUB
    if tall:
        block_hbm, *block_refs, block_ref = block_refs
        block_refs = [block_ref, *block_refs]
    outs = []

    def put(value, start):
        put_blocks(block_refs, value, start)
        if tall:
            send_columns(block_ref, block_hbm, out_sems, outs, start, half)

    copies = [
        pltpu.make_async_copy(rows_hbm.at[:, pl.ds(c, half)], rows_ref.at[:, pl.ds(c, half)], sems.at[c // half])
        for c in (0, half)
    ]
    for copy in copies:
        copy.start()
    tail = jnp.zeros((height, half), F32)
    for copy, c in zip(copies, (0, half), strict=True):
        copy.wait()
        got = t_dot(hit_ref[...], rows_ref[:, c : c + half])
        for n in range(SLABS):
            put(got[n * height : (n + 1) * height], n * features + c)
        tail += half_rows(got[SLABS * height :], c > 0)
    put(tail, SLABS * features)
    for copy in outs:
        copy.wait()


def combine_kernel(*refs):
    *block_refs, line_ref, out_ref, block_ref = refs
    stack_blocks(block_refs, block_ref)
    half = out_ref.shape[1] // 2
    for c in (0, half):
        out_ref[:, c : c + half] = t_dot(line_ref[...], half_right(block_ref, c > 0)).astype(BF16)


def true_rows(where_ref, row, part, each, cap):
    y, z_hi = where_ref[4], where_ref[5]
    sender = over(row, each)
    inside = row - sender * each
    q = over(inside, cap)
    slot = inside - q * cap
    z = z_hi * 2 + sender % 2
    up = jnp.where(sender % 2 == 1, 1, -1)
    if part == 0:
        sources = 12
        odd = jnp.where(sender % 2 == 1, z, z - 1)
        z = jnp.where(q < 4, odd, jnp.where(q < 8, odd + 1, z + 2 * up))
        at_y = jnp.where(q < 8, q, y - q + 4 * NY)
    else:
        sources = 4
        z = z + 3 * up
        at_y = y - q + 4 * NY
    z = (z + NZ) % NZ
    source = (((z // 2) * NY + at_y % NY) * NX + sender // 2) * 2 + z % 2
    return jnp.where(q < sources, source * cap + slot, -1)


def align_kernel(dims, where_ref, saved_ref, *part_refs):
    in_group, cap = dims
    slots = saved_ref.shape[0]
    for part, ref in enumerate(part_refs):
        rows = ref.shape[0]
        true = true_rows(where_ref, iota((rows, 1), 0), part, rows // in_group, cap)
        ref[...] = dot(flag(true == iota((rows, slots), 1)), saved_ref[...]).astype(BF16)


def restore_kernel(dims, where_ref, *refs):
    in_group, cap = dims
    *part_refs, out_ref = refs
    slots = out_ref.shape[0]
    total = jnp.zeros(out_ref.shape, F32)
    for part, ref in enumerate(part_refs):
        rows = ref.shape[0]
        true = true_rows(where_ref, iota((1, rows), 1), part, rows // in_group, cap)
        total += dot(flag(true == iota((slots, rows), 0)), ref[...])
    out_ref[...] = total.astype(BF16)


def expert_kernel(held, x_hbm, kept_hbm, wd_hbm, wu_hbm, out_hbm, gate_hbm, x_ref, kept_ref, wd_ref, wu_ref, up_ref, out_ref, gate_ref, sems):
    hidden, features = wd_ref.shape
    rows = x_ref.shape[0]
    step, wide, tall = hidden // 3, features // 5, rows // 2 if rows > 256 else rows
    count = iter(range(sems.shape[0]))

    def copy(source, target, index):
        return pltpu.make_async_copy(source.at[index], target.at[index], sems.at[next(count)])

    tops = [pl.ds(r, tall) for r in range(0, rows, tall)]
    x = [] if held else [copy(x_hbm, x_ref, t) for t in tops]
    x_ref = x_hbm if held else x_ref
    kept = [copy(kept_hbm, kept_ref, t) for t in tops]
    down = [copy(wd_hbm, wd_ref, pl.ds(n, step)) for n in range(0, hidden, step)]
    up = [copy(wu_hbm, wu_ref, pl.ds(n, wide)) for n in range(0, features, wide)]
    for c in (*x[:1], down[0], kept[0], *down[1:], *x[1:], *kept[1:], *up):
        c.start()
    out = []
    for i, r in enumerate(range(0, rows, tall)):
        if not held:
            x[i].wait()
        for j, n in enumerate(range(0, hidden, step)):
            if i == 0:
                down[j].wait()
            grad = dot_t(x_ref[r : r + tall, :], wd_ref[n : n + step, :])
            if j == 0:
                kept[i].wait()
            act = kept_ref[r : r + tall, n : n + step].astype(F32)
            up_ref[r : r + tall, n : n + step] = (grad * act).astype(BF16)
            value = kept_ref[r : r + tall, hidden + n : hidden + n + step].astype(F32)
            gate_ref[r : r + tall, n : n + step] = (grad * value).astype(BF16)
        out.append(copy(gate_ref, gate_hbm, tops[i]))
        out[-1].start()
    for i, n in enumerate(range(0, features, wide)):
        up[i].wait()
        out_ref[:, n : n + wide] = dot_t(up_ref[...], wu_ref[n : n + wide, :]).astype(BF16)
        out.append(copy(out_ref, out_hbm, (slice(None), pl.ds(n, wide))))
        out[-1].start()
    for c in out:
        c.wait()


def device_at(z, y, x):
    return (((z // 2) % (NZ // 2) * NY + y % NY) * NX + x) * 2 + z % 2


PAIR_SETS = [
    [device_at(z % NZ, y, x) for z in (odd, odd + 1) for y in range(NY)]
    for x in range(NX)
    for odd in range(1, NZ, 2)
]


def routes_over(hops, dy, back):
    pairs = []
    for z in range(NZ):
        to = (z + (hops if (z % 2 == 1) == (hops == 3) else -hops)) % NZ
        pairs += [(device_at(z, y, x), device_at(to, y + dy, x)) for y in range(NY) for x in range(NX)]
    return [(b, a) for a, b in pairs] if back else pairs


def on_device(grad_out, route_ids, route_w, saved, w_up, w_down):
    both = ("outer", "inner")
    groups, in_group = lax.axis_size("outer"), lax.axis_size("inner")
    tok, features = grad_out.shape[1:]
    routes = route_ids.shape[2]
    slots_all = saved.shape[2]
    cap = slots_all // (groups * in_group)
    hidden = w_up.shape[3]
    group_cap = max(2, 7 * tok * ROUTE_GROUPS // (6 * groups))
    wide = SLABS * features + features // 2
    sent = wide + FIELDS
    deep = (SLABS + 1) * BLOCKS * SUB
    heights = [in_group * -(-(sources * cap) // SUB) * SUB for sources in (12, 4)]
    outer, inner = lax.axis_index("outer"), lax.axis_index("inner")
    z_hi, y, z_lo = outer // NY, outer % NY, inner % 2
    z = z_hi * 2 + z_lo
    up = 2 * z_lo - 1
    odd = (z + z_lo - 1) % NZ
    where = jnp.stack([odd, (odd + 1) % NZ, (z - 2 * up) % NZ, (z + 3 * up) % NZ, y, z_hi]).astype(I32)
    vmem, hbm = pl.BlockSpec(memory_space=pltpu.VMEM), pl.BlockSpec(memory_space=pltpu.HBM)
    smem = pl.BlockSpec(memory_space=pltpu.SMEM)

    def array(*shape):
        return jax.ShapeDtypeStruct(shape, BF16)

    def call(kernel, name, n_in, outs, mib, flops, out_specs=None, scratch=(), scalars=True):
        moved = 2 * sum(functools.reduce(lambda a, b: a * b, o.shape) for o in outs)
        return pl.pallas_call(
            kernel,
            name=name,
            in_specs=[smem] * scalars + [vmem] * n_in,
            out_specs=out_specs or [vmem] * len(outs),
            out_shape=list(outs),
            scratch_shapes=list(scratch),
            compiler_params=pltpu.CompilerParams(vmem_limit_bytes=mib * 2**20),
            cost_estimate=pl.CostEstimate(flops=flops, bytes_accessed=moved, transcendentals=0),
        )

    def near_swap(block):
        width = block.shape[1]
        moved = lax.all_to_all(block.reshape(8, SUB, width), both, 0, 0, axis_index_groups=PAIR_SETS, tiled=True)
        return moved.reshape(8 * SUB, width)

    def hop(blocks, hops, back=False):
        return [lax.ppermute(b, both, routes_over(hops, dy, back)) for dy, b in enumerate(blocks)]

    def in_groups(rows):
        moved = lax.all_to_all(rows.reshape(in_group, -1, features), "inner", 0, 0, tiled=True)
        return moved.reshape(rows.shape)

    def spread(name, blocks, rows):
        height = sum(b.shape[0] for b in blocks)
        depth = (SLABS + 1) * height
        return call(
            functools.partial(spread_kernel, (in_group, cap)), name, len(blocks),
            [array(rows, features), array(rows, depth)], 48, 2 * rows * depth * features,
            [hbm, vmem],
            [pltpu.VMEM((height, sent), BF16), pltpu.VMEM((rows, features), BF16), pltpu.SemaphoreType.DMA((2,))],
            scalars=False,
        )(*blocks)

    def gather(name, rows, hit, shapes):
        return pl.pallas_call(
            gather_kernel,
            name=name,
            in_specs=[hbm, vmem],
            out_specs=[hbm if h > SUB else vmem for h in shapes],
            out_shape=[array(h, wide) for h in shapes],
            scratch_shapes=[
                *(pltpu.VMEM((h, wide), BF16) for h in shapes if h > SUB),
                pltpu.VMEM(rows.shape, BF16),
                pltpu.SemaphoreType.DMA((2,)),
                pltpu.SemaphoreType.DMA((2 * SLABS + 1,)),
            ],
            compiler_params=pltpu.CompilerParams(vmem_limit_bytes=20 * 2**20),
            cost_estimate=pl.CostEstimate(
                flops=2 * hit.shape[0] * hit.shape[1] * features, bytes_accessed=2 * rows.shape[0] * features, transcendentals=0
            ),
        )(rows, hit)

    def after(first, *values):
        *values, first = lax.optimization_barrier((*values, first))
        return first, *values

    ids, weights = (jnp.transpose(a, (2, 0, 1)) for a in (route_ids, route_w))
    shapes = [8 * SUB] + [SUB] * 8
    near, *others = call(
        functools.partial(dispatch_kernel, (groups, in_group, group_cap, cap)), "dispatch", 3,
        [array(h, sent) for h in shapes], 12, 2 * deep * tok * features, [hbm] + [vmem] * 8,
        [pltpu.VMEM((8 * SUB, sent), BF16), pltpu.SemaphoreType.DMA((2 * SLABS + 2,))],
    )(where, ids, weights, grad_out[0])
    [line] = call(
        functools.partial(lines_kernel, (groups, in_group, group_cap)), "lines", 1,
        [array(deep, tok)], 8, 4 * deep * tok * tok,
    )(where, ids)
    kept = call(
        functools.partial(align_kernel, (in_group, cap)), "align", 1, [array(h, 2 * hidden) for h in heights], 16,
        4 * sum(heights) * slots_all * hidden,
    )(where, saved[0, 0])

    near, mid, far = near_swap(near), hop(others[:4], 2), others[4:]
    near, *ready = after(near, *mid, *far)
    mid, far = ready[:4], hop(ready[4:], 3)
    rows_n, hit_n = spread("spread_near", [near, *mid], heights[0])
    rows_n = in_groups(rows_n)
    rows_f, hit_f = spread("spread_far", far, heights[1])
    rows_n, rows_f = after(rows_n, rows_f)
    rows_f = in_groups(rows_f)
    rows_n, gate_n = expert_call("expert_near", rows_n, kept[0], w_down[0, 0], w_up[0, 0])
    rows_f, gate_f = expert_call("expert_far", rows_f, kept[1], w_down[0, 0], w_up[0, 0])
    rows_f = in_groups(rows_f)
    far = gather("gather_far", rows_f, hit_f, [SUB] * 4)
    rows_n, *far = after(rows_n, *far)
    far = hop(far, 3, True)
    rows_n = in_groups(rows_n)
    rows_n, *far = after(rows_n, *far)
    [gate_grad] = call(
        functools.partial(restore_kernel, (in_group, cap)), "restore", 2, [array(slots_all, hidden)], 12,
        2 * sum(heights) * slots_all * hidden,
    )(where, gate_n, gate_f)
    near, *mid = gather("gather_near", rows_n, hit_n, [8 * SUB] + [SUB] * 4)
    near, mid = near_swap(near), hop(mid, 2, True)
    gate_grad, line = after(gate_grad, line)
    [token_grad] = call(
        combine_kernel, "combine", 10, [array(tok, features)], 12, 2 * deep * tok * features,
        scratch=[pltpu.VMEM((BLOCKS * SUB, wide), BF16)], scalars=False,
    )(near, *mid, *far, line)
    count = lax.axis_size("section")
    received = lax.ppermute(token_grad, "section", [((i + 1) % count, i) for i in range(count)])
    return (received[None], gate_grad[None, None])


def expert_call(name, rows, kept, w_down, w_up):
    hidden, features = w_down.shape
    height = rows.shape[0]
    vmem, hbm = pl.BlockSpec(memory_space=pltpu.VMEM), pl.BlockSpec(memory_space=pltpu.HBM)
    held = height <= 256
    return pl.pallas_call(
        functools.partial(expert_kernel, held),
        name=name,
        in_specs=[vmem if held else hbm] + [hbm] * 3,
        out_specs=[hbm] * 2,
        out_shape=[jax.ShapeDtypeStruct((height, features), BF16), jax.ShapeDtypeStruct((height, hidden), BF16)],
        scratch_shapes=[
            pltpu.VMEM((height, features), BF16),
            pltpu.VMEM((height, 2 * hidden), BF16),
            pltpu.VMEM((hidden, features), BF16),
            pltpu.VMEM((features, hidden), BF16),
            pltpu.VMEM((height, hidden), BF16),
            pltpu.VMEM((height, features), BF16),
            pltpu.VMEM((height, hidden), BF16),
            pltpu.SemaphoreType.DMA((19,)),
        ],
        compiler_params=pltpu.CompilerParams(vmem_limit_bytes=(51 if held else 56) * 2**20),
        cost_estimate=pl.CostEstimate(
            flops=4 * height * features * hidden, bytes_accessed=4 * (height + hidden) * features, transcendentals=0
        ),
    )(rows, kept, w_down, w_up)


def solution(mesh):
    return jax.shard_map(
        on_device,
        mesh=mesh,
        in_specs=(
            P("section", ("outer", "inner"), None),
            P("section", ("outer", "inner"), None),
            P("section", ("outer", "inner"), None),
            P("section", ("outer", "inner"), None, None),
            P("section", ("outer", "inner"), None, None),
            P("section", ("outer", "inner"), None, None),
        ),
        out_specs=(
            P("section", ("outer", "inner"), None),
            P("section", ("outer", "inner"), None, None),
        ),
        check_vma=False,
    )
```

```python
import functools
import jax
import jax.numpy as jnp
from jax import lax
from jax.experimental import pallas as pl
from jax.experimental.pallas import tpu as pltpu
from jax.sharding import PartitionSpec as P

NZ, NY, NX = 8, 4, 4
ROUTE_GROUPS = 3
SUB = 8
SLABS = 3
FIELDS = 128
BLOCKS = 16
F32 = jnp.float32
BF16 = jnp.bfloat16
I32 = jnp.int32


def iota(shape, dim):
    return lax.broadcasted_iota(I32, shape, dim)


def dot(a, b):
    return lax.dot_general(a, b, (((1,), (0,)), ((), ())), preferred_element_type=F32)


def dot_t(a, b):
    return lax.dot_general(a, b, (((1,), (1,)), ((), ())), preferred_element_type=F32)


def t_dot(a, b):
    return lax.dot_general(a, b, (((0,), (0,)), ((), ())), preferred_element_type=F32)


def flag(mask, kind=BF16):
    return jnp.where(mask, 1.0, 0.0).astype(kind)


def over(value, divisor):
    return jnp.floor((value.astype(F32) + 0.5) * (1.0 / divisor)).astype(I32)


def top_bits(value):
    wide = value * 65537.0
    return wide - (wide - value)


def block_group(where_ref, block):
    odd, even, mid, far, y = (where_ref[i] for i in range(5))
    z = jnp.where(block < 4, odd, jnp.where(block < 8, even, jnp.where(block < 12, mid, far)))
    return (z // 2) * NY + jnp.where(block < 8, block % NY, (block + y) % NY)


def slots_in_group(member, group_cap):
    tok = member.shape[1]
    before = flag(iota((tok, tok), 0) < iota((tok, tok), 1))
    rank = dot(member.astype(BF16), before)
    return jnp.where((member > 0) & (rank < group_cap), rank, -1.0)


def token_lines(where_ref, group_slot):
    groups, tok = group_slot.shape
    rows = (SLABS + 1) * BLOCKS * SUB
    r = iota((rows, groups), 0)
    chosen = flag(block_group(where_ref, (r // SUB) % BLOCKS) == iota((rows, groups), 1))
    r = iota((rows, tok), 0)
    slab, sub = r // (BLOCKS * SUB), r % SUB
    slot = jnp.where(slab == SLABS, SLABS * SUB + sub % 4, slab * SUB + sub)
    return flag(dot(chosen, group_slot.astype(BF16)) == slot.astype(F32))


def half_rows(value, second):
    sub = iota(value.shape, 0) % SUB
    return jnp.where(sub >= 4 if second else sub < 4, value, jnp.zeros_like(value))


def half_right(block_ref, second):
    features = block_ref.shape[1] // (2 * SLABS + 1) // FIELDS * FIELDS * 2
    half, tail = features // 2, SLABS * features
    c = half if second else 0
    last = half_rows(block_ref[:, tail : tail + half].astype(F32), second).astype(BF16)
    return jnp.concatenate([*(block_ref[:, n * features + c : n * features + c + half] for n in range(SLABS)), last], axis=0)


def lines_kernel(dims, where_ref, ids_ref, line_ref):
    groups, in_group, group_cap = dims
    routes, _, tok = ids_ref.shape
    member = jnp.zeros((groups, tok), F32)
    for k in range(0, routes, routes // ROUTE_GROUPS):
        member += flag(ids_ref[k] // in_group == iota((groups, tok), 0), F32)
    line_ref[...] = token_lines(where_ref, slots_in_group(member, group_cap))


def send_columns(block_ref, block_hbm, sems, copies, start, width):
    columns = (slice(None), pl.ds(start, width))
    copies.append(pltpu.make_async_copy(block_ref.at[columns], block_hbm.at[columns], sems.at[len(copies)]))
    copies[-1].start()


def put_blocks(block_refs, value, start):
    row = 0
    for ref in block_refs:
        ref[:, start : start + value.shape[1]] = value[row : row + ref.shape[0]].astype(BF16)
        row += ref.shape[0]


def stack_blocks(block_refs, stacked_ref):
    width, row, first = stacked_ref.shape[1], 0, None
    for ref in block_refs:
        if ref.shape[0] > SUB:
            stacked_ref[row : row + ref.shape[0], :] = ref[:, :width]
            row += ref.shape[0]
        elif first is None:
            first = ref
        else:
            pair = jnp.concatenate([first[:, :width].astype(F32), ref[:, :width].astype(F32)], axis=0)
            stacked_ref[row : row + 2 * SUB, :] = pair.astype(BF16)
            row, first = row + 2 * SUB, None


def dispatch_kernel(dims, where_ref, ids_ref, w_ref, g_ref, near_hbm, *refs):
    *block_refs, near_ref, sems = refs
    block_refs, copies = [near_ref, *block_refs], []
    groups, in_group, group_cap, cap = dims
    routes, _, tok = ids_ref.shape
    features, experts = g_ref.shape[1], groups * in_group
    half, per = features // 2, routes // ROUTE_GROUPS
    e, group = iota((experts, tok), 0), iota((groups, tok), 0)
    before = flag(iota((tok, tok), 0) < iota((tok, tok), 1))
    ids = [ids_ref[k] for k in range(routes)]
    named = jnp.zeros((experts, tok), F32)
    mine = jnp.zeros((experts, tok), F32)
    member = jnp.zeros((groups, tok), F32)
    for k in range(routes):
        named += flag(ids[k] == e, F32)
        if k % per == 0:
            mine += flag(ids[k] // in_group == e // in_group, F32)
            member += flag(ids[k] // in_group == group, F32)
    admitted = (named > 0) & (dot(mine.astype(BF16), before) < group_cap)
    slot_rank = dot(flag(admitted), before)
    rank = jnp.where(admitted & (slot_rank < cap), slot_rank, -1.0)
    group_slot = slots_in_group(member, group_cap)
    fields = [jnp.zeros((groups, tok), F32) for _ in range(SUB)]
    for k in range(routes):
        own = jnp.sum(jnp.where(ids[k] == e, rank, 0.0), axis=0, keepdims=True)
        place = jnp.where(own >= 0, (ids[k] % in_group).astype(F32) * cap + own + 1.0, 0.0)
        weight = w_ref[k]
        first = top_bits(weight)
        second = top_bits(weight - first)
        third = (weight - first) - second
        at = ids[k] // in_group == group
        for f, value in ((k % per, place), *((per + 3 * (k % per) + i, v) for i, v in enumerate((first, second, third)))):
            fields[f] += jnp.where(at, value, 0.0)
    stacked = jnp.concatenate([f.astype(BF16) for f in fields], axis=0)
    line = token_lines(where_ref, group_slot)
    rows, part = line.shape[0], groups * SUB
    r, c = iota((part, part), 0), iota((part, part), 1)
    choose = flag((block_group(where_ref, r // SUB) == c % groups) & (r % SUB == c // groups))
    by_block = dot(choose, stacked).astype(BF16)
    by_slot = dot_t(by_block, line)
    r, c = iota((part, rows), 0), iota((part, rows), 1)
    by_slot = jnp.where((c // SUB) % groups == r // SUB, by_slot, 0.0).astype(BF16)
    r, c = iota((rows, FIELDS), 0), iota((rows, FIELDS), 1)
    fold = flag(c == (r // part) * SUB + r % SUB)
    block_fields = dot(by_slot, fold)

    def put(value, start, width):
        put_blocks(block_refs, value, start)
        send_columns(near_ref, near_hbm, sems, copies, start, width)

    for n in range(SLABS):
        for c in (0, half):
            put(dot(line[n * part : (n + 1) * part], g_ref[:, c : c + half]), n * features + c, half)
    line = line[SLABS * part :]
    put(
        half_rows(dot(line, g_ref[:, :half]), False) + half_rows(dot(line, g_ref[:, half:]), True),
        SLABS * features, half,
    )
    put(block_fields, SLABS * features + half, FIELDS)
    for copy in copies:
        copy.wait()


def spread_kernel(dims, *refs):
    *block_refs, out_hbm, hit_ref, block_ref, out_ref, sems = refs
    stack_blocks(block_refs, block_ref)
    in_group, cap = dims
    height, features = block_ref.shape[0], out_ref.shape[1]
    sources = height // SUB
    half, tail = features // 2, SLABS * features

    deep = (SLABS + 1) * height
    l, c = iota((FIELDS, deep), 0), iota((FIELDS, deep), 1)
    unfold = flag((l == (c // height) * SUB + c % SUB) & (l < (SLABS + 1) * SUB))
    wide = dot(block_ref[:, tail + half :], unfold)
    r, c = iota((height, deep), 0), iota((height, deep), 1)
    wide = jnp.where(r // SUB == (c // SUB) % sources, wide, 0.0)
    fields = wide[:SUB]
    for q in range(1, sources):
        fields += wide[q * SUB : (q + 1) * SUB]
    places = [fields[k : k + 1].astype(I32) for k in range(2)]
    weights = [(fields[2 + 3 * k : 3 + 3 * k] + fields[3 + 3 * k : 4 + 3 * k]) + fields[4 + 3 * k : 5 + 3 * k] for k in range(2)]
    rows = out_ref.shape[0]
    s = iota((rows, 1), 0)
    each = rows // in_group
    expert = over(s, each)
    inside = s - expert * each
    source = over(inside, cap)
    key = source * 64 + expert * cap + (inside - source * cap) + 1
    key = jnp.where(source < sources, key, -2)
    c = iota((1, deep), 1)
    base = ((c // SUB) % sources) * 64
    hits = [key == jnp.where(place > 0, base + place, -1) for place in places]
    once = iota((1, deep), 1)
    once = (once < SLABS * height) | (once % SUB < 4)
    hit_ref[...] = flag(hits[0] | hits[1])
    scale = jnp.where(hits[0], jnp.where(once, weights[0], 0.0), 0.0)
    scale += jnp.where(hits[1], jnp.where(once, weights[1], 0.0), 0.0)
    scale = jnp.sum(scale, axis=1, keepdims=True)
    copies = []
    for c in (0, half):
        out_ref[:, c : c + half] = (dot(hit_ref[...], half_right(block_ref, c > 0)) * scale).astype(BF16)
        copies.append(
            pltpu.make_async_copy(out_ref.at[:, pl.ds(c, half)], out_hbm.at[:, pl.ds(c, half)], sems.at[c // half])
        )
        copies[-1].start()
    for copy in copies:
        copy.wait()


def gather_kernel(rows_hbm, hit_ref, *refs):
    *block_refs, rows_ref, sems, out_sems = refs
    features, height = rows_ref.shape[1], hit_ref.shape[1] // (SLABS + 1)
    half = features // 2
    tall = block_refs[0].shape[0] > SUB
    if tall:
        block_hbm, *block_refs, block_ref = block_refs
        block_refs = [block_ref, *block_refs]
    outs = []

    def put(value, start):
        put_blocks(block_refs, value, start)
        if tall:
            send_columns(block_ref, block_hbm, out_sems, outs, start, half)

    copies = [
        pltpu.make_async_copy(rows_hbm.at[:, pl.ds(c, half)], rows_ref.at[:, pl.ds(c, half)], sems.at[c // half])
        for c in (0, half)
    ]
    for copy in copies:
        copy.start()
    tail = jnp.zeros((height, half), F32)
    for copy, c in zip(copies, (0, half), strict=True):
        copy.wait()
        got = t_dot(hit_ref[...], rows_ref[:, c : c + half])
        for n in range(SLABS):
            put(got[n * height : (n + 1) * height], n * features + c)
        tail += half_rows(got[SLABS * height :], c > 0)
    put(tail, SLABS * features)
    for copy in outs:
        copy.wait()


def combine_kernel(*refs):
    *block_refs, line_ref, out_ref, block_ref = refs
    stack_blocks(block_refs, block_ref)
    half = out_ref.shape[1] // 2
    for c in (0, half):
        out_ref[:, c : c + half] = t_dot(line_ref[...], half_right(block_ref, c > 0)).astype(BF16)


def true_rows(where_ref, row, part, each, cap):
    y, z_hi = where_ref[4], where_ref[5]
    sender = over(row, each)
    inside = row - sender * each
    q = over(inside, cap)
    slot = inside - q * cap
    z = z_hi * 2 + sender % 2
    up = jnp.where(sender % 2 == 1, 1, -1)
    if part == 0:
        sources = 12
        odd = jnp.where(sender % 2 == 1, z, z - 1)
        z = jnp.where(q < 4, odd, jnp.where(q < 8, odd + 1, z + 2 * up))
        at_y = jnp.where(q < 8, q, y - q + 4 * NY)
    else:
        sources = 4
        z = z + 3 * up
        at_y = y - q + 4 * NY
    z = (z + NZ) % NZ
    source = (((z // 2) * NY + at_y % NY) * NX + sender // 2) * 2 + z % 2
    return jnp.where(q < sources, source * cap + slot, -1)


def align_kernel(dims, where_ref, saved_ref, *part_refs):
    in_group, cap = dims
    slots = saved_ref.shape[0]
    for part, ref in enumerate(part_refs):
        rows = ref.shape[0]
        true = true_rows(where_ref, iota((rows, 1), 0), part, rows // in_group, cap)
        ref[...] = dot(flag(true == iota((rows, slots), 1)), saved_ref[...]).astype(BF16)


def restore_kernel(dims, where_ref, *refs):
    in_group, cap = dims
    *part_refs, out_ref = refs
    slots = out_ref.shape[0]
    total = jnp.zeros(out_ref.shape, F32)
    for part, ref in enumerate(part_refs):
        rows = ref.shape[0]
        true = true_rows(where_ref, iota((1, rows), 1), part, rows // in_group, cap)
        total += dot(flag(true == iota((slots, rows), 0)), ref[...])
    out_ref[...] = total.astype(BF16)


def expert_kernel(held, x_hbm, kept_hbm, wd_hbm, wu_hbm, out_hbm, gate_hbm, x_ref, kept_ref, wd_ref, wu_ref, up_ref, out_ref, gate_ref, sems):
    hidden, features = wd_ref.shape
    rows = x_ref.shape[0]
    step, wide, tall = hidden // 3, features // 5, rows // 2 if rows > 256 else rows
    count = iter(range(sems.shape[0]))

    def copy(source, target, index):
        return pltpu.make_async_copy(source.at[index], target.at[index], sems.at[next(count)])

    tops = [pl.ds(r, tall) for r in range(0, rows, tall)]
    x = [] if held else [copy(x_hbm, x_ref, t) for t in tops]
    x_ref = x_hbm if held else x_ref
    kept = [copy(kept_hbm, kept_ref, t) for t in tops]
    down = [copy(wd_hbm, wd_ref, pl.ds(n, step)) for n in range(0, hidden, step)]
    up = [copy(wu_hbm, wu_ref, pl.ds(n, wide)) for n in range(0, features, wide)]
    for c in (*x[:1], down[0], kept[0], *down[1:], *x[1:], *kept[1:], *up):
        c.start()
    out = []
    for i, r in enumerate(range(0, rows, tall)):
        if not held:
            x[i].wait()
        for j, n in enumerate(range(0, hidden, step)):
            if i == 0:
                down[j].wait()
            grad = dot_t(x_ref[r : r + tall, :], wd_ref[n : n + step, :])
            if j == 0:
                kept[i].wait()
            act = kept_ref[r : r + tall, n : n + step].astype(F32)
            up_ref[r : r + tall, n : n + step] = (grad * act).astype(BF16)
            value = kept_ref[r : r + tall, hidden + n : hidden + n + step].astype(F32)
            gate_ref[r : r + tall, n : n + step] = (grad * value).astype(BF16)
        out.append(copy(gate_ref, gate_hbm, tops[i]))
        out[-1].start()
    for i, n in enumerate(range(0, features, wide)):
        up[i].wait()
        out_ref[:, n : n + wide] = dot_t(up_ref[...], wu_ref[n : n + wide, :]).astype(BF16)
        out.append(copy(out_ref, out_hbm, (slice(None), pl.ds(n, wide))))
        out[-1].start()
    for c in out:
        c.wait()


def device_at(z, y, x):
    return (((z // 2) % (NZ // 2) * NY + y % NY) * NX + x) * 2 + z % 2


PAIR_SETS = [
    [device_at(z % NZ, y, x) for z in (odd, odd + 1) for y in range(NY)]
    for x in range(NX)
    for odd in range(1, NZ, 2)
]


def routes_over(hops, dy, back):
    pairs = []
    for z in range(NZ):
        to = (z + (hops if (z % 2 == 1) == (hops == 3) else -hops)) % NZ
        pairs += [(device_at(z, y, x), device_at(to, y + dy, x)) for y in range(NY) for x in range(NX)]
    return [(b, a) for a, b in pairs] if back else pairs


def on_device(grad_out, route_ids, route_w, saved, w_up, w_down):
    both = ("outer", "inner")
    groups, in_group = lax.axis_size("outer"), lax.axis_size("inner")
    tok, features = grad_out.shape[1:]
    routes = route_ids.shape[2]
    slots_all = saved.shape[2]
    cap = slots_all // (groups * in_group)
    hidden = w_up.shape[3]
    group_cap = max(2, 7 * tok * ROUTE_GROUPS // (6 * groups))
    wide = SLABS * features + features // 2
    sent = wide + FIELDS
    deep = (SLABS + 1) * BLOCKS * SUB
    heights = [in_group * -(-(sources * cap) // SUB) * SUB for sources in (12, 4)]
    outer, inner = lax.axis_index("outer"), lax.axis_index("inner")
    z_hi, y, z_lo = outer // NY, outer % NY, inner % 2
    z = z_hi * 2 + z_lo
    up = 2 * z_lo - 1
    odd = (z + z_lo - 1) % NZ
    where = jnp.stack([odd, (odd + 1) % NZ, (z - 2 * up) % NZ, (z + 3 * up) % NZ, y, z_hi]).astype(I32)
    vmem, hbm = pl.BlockSpec(memory_space=pltpu.VMEM), pl.BlockSpec(memory_space=pltpu.HBM)
    smem = pl.BlockSpec(memory_space=pltpu.SMEM)

    def array(*shape):
        return jax.ShapeDtypeStruct(shape, BF16)

    def call(kernel, name, n_in, outs, mib, flops, out_specs=None, scratch=(), scalars=True):
        moved = 2 * sum(functools.reduce(lambda a, b: a * b, o.shape) for o in outs)
        return pl.pallas_call(
            kernel,
            name=name,
            in_specs=[smem] * scalars + [vmem] * n_in,
            out_specs=out_specs or [vmem] * len(outs),
            out_shape=list(outs),
            scratch_shapes=list(scratch),
            compiler_params=pltpu.CompilerParams(vmem_limit_bytes=mib * 2**20),
            cost_estimate=pl.CostEstimate(flops=flops, bytes_accessed=moved, transcendentals=0),
        )

    def near_swap(block):
        width = block.shape[1]
        moved = lax.all_to_all(block.reshape(8, SUB, width), both, 0, 0, axis_index_groups=PAIR_SETS, tiled=True)
        return moved.reshape(8 * SUB, width)

    def hop(blocks, hops, back=False):
        return [lax.ppermute(b, both, routes_over(hops, dy, back)) for dy, b in enumerate(blocks)]

    def in_groups(rows):
        moved = lax.all_to_all(rows.reshape(in_group, -1, features), "inner", 0, 0, tiled=True)
        return moved.reshape(rows.shape)

    def spread(name, blocks, rows):
        height = sum(b.shape[0] for b in blocks)
        depth = (SLABS + 1) * height
        return call(
            functools.partial(spread_kernel, (in_group, cap)), name, len(blocks),
            [array(rows, features), array(rows, depth)], 52 if rows > 256 else 48, 2 * rows * depth * features,
            [hbm, vmem],
            [pltpu.VMEM((height, sent), BF16), pltpu.VMEM((rows, features), BF16), pltpu.SemaphoreType.DMA((2,))],
            scalars=False,
        )(*blocks)

    def gather(name, rows, hit, shapes):
        return pl.pallas_call(
            gather_kernel,
            name=name,
            in_specs=[hbm, vmem],
            out_specs=[hbm if h > SUB else vmem for h in shapes],
            out_shape=[array(h, wide) for h in shapes],
            scratch_shapes=[
                *(pltpu.VMEM((h, wide), BF16) for h in shapes if h > SUB),
                pltpu.VMEM(rows.shape, BF16),
                pltpu.SemaphoreType.DMA((2,)),
                pltpu.SemaphoreType.DMA((2 * SLABS + 1,)),
            ],
            compiler_params=pltpu.CompilerParams(vmem_limit_bytes=20 * 2**20),
            cost_estimate=pl.CostEstimate(
                flops=2 * hit.shape[0] * hit.shape[1] * features, bytes_accessed=2 * rows.shape[0] * features, transcendentals=0
            ),
        )(rows, hit)

    def after(first, *values):
        *values, first = lax.optimization_barrier((*values, first))
        return first, *values

    ids, weights = (jnp.transpose(a, (2, 0, 1)) for a in (route_ids, route_w))
    shapes = [8 * SUB] + [SUB] * 8
    near, *others = call(
        functools.partial(dispatch_kernel, (groups, in_group, group_cap, cap)), "dispatch", 3,
        [array(h, sent) for h in shapes], 12, 2 * deep * tok * features, [hbm] + [vmem] * 8,
        [pltpu.VMEM((8 * SUB, sent), BF16), pltpu.SemaphoreType.DMA((2 * SLABS + 2,))],
    )(where, ids, weights, grad_out[0])
    [line] = call(
        functools.partial(lines_kernel, (groups, in_group, group_cap)), "lines", 1,
        [array(deep, tok)], 8, 4 * deep * tok * tok,
    )(where, ids)
    kept = call(
        functools.partial(align_kernel, (in_group, cap)), "align", 1, [array(h, 2 * hidden) for h in heights], 16,
        4 * sum(heights) * slots_all * hidden,
    )(where, saved[0, 0])

    near, mid, far = near_swap(near), hop(others[:4], 2), others[4:]
    near, *ready = after(near, *mid, *far)
    mid, far = ready[:4], hop(ready[4:], 3)
    rows_n, hit_n = spread("spread_near", [near, *mid], heights[0])
    rows_n = in_groups(rows_n)
    rows_f, hit_f = spread("spread_far", far, heights[1])
    rows_n, rows_f = after(rows_n, rows_f)
    rows_f = in_groups(rows_f)
    rows_n, gate_n = expert_call("expert_near", rows_n, kept[0], w_down[0, 0], w_up[0, 0])
    rows_f, gate_f = expert_call("expert_far", rows_f, kept[1], w_down[0, 0], w_up[0, 0])
    rows_f = in_groups(rows_f)
    far = gather("gather_far", rows_f, hit_f, [SUB] * 4)
    rows_n, *far = after(rows_n, *far)
    far = hop(far, 3, True)
    rows_n = in_groups(rows_n)
    rows_n, *far = after(rows_n, *far)
    [gate_grad] = call(
        functools.partial(restore_kernel, (in_group, cap)), "restore", 2, [array(slots_all, hidden)], 12,
        2 * sum(heights) * slots_all * hidden,
    )(where, gate_n, gate_f)
    near, *mid = gather("gather_near", rows_n, hit_n, [8 * SUB] + [SUB] * 4)
    near, mid = near_swap(near), hop(mid, 2, True)
    gate_grad, line = after(gate_grad, line)
    [token_grad] = call(
        combine_kernel, "combine", 10, [array(tok, features)], 12, 2 * deep * tok * features,
        scratch=[pltpu.VMEM((BLOCKS * SUB, wide), BF16)], scalars=False,
    )(near, *mid, *far, line)
    count = lax.axis_size("section")
    received = lax.ppermute(token_grad, "section", [((i + 1) % count, i) for i in range(count)])
    return (received[None], gate_grad[None, None])


def expert_call(name, rows, kept, w_down, w_up):
    hidden, features = w_down.shape
    height = rows.shape[0]
    vmem, hbm = pl.BlockSpec(memory_space=pltpu.VMEM), pl.BlockSpec(memory_space=pltpu.HBM)
    held = height <= 256
    return pl.pallas_call(
        functools.partial(expert_kernel, held),
        name=name,
        in_specs=[vmem if held else hbm] + [hbm] * 3,
        out_specs=[hbm] * 2,
        out_shape=[jax.ShapeDtypeStruct((height, features), BF16), jax.ShapeDtypeStruct((height, hidden), BF16)],
        scratch_shapes=[
            pltpu.VMEM((height, features), BF16),
            pltpu.VMEM((height, 2 * hidden), BF16),
            pltpu.VMEM((hidden, features), BF16),
            pltpu.VMEM((features, hidden), BF16),
            pltpu.VMEM((height, hidden), BF16),
            pltpu.VMEM((height, features), BF16),
            pltpu.VMEM((height, hidden), BF16),
            pltpu.SemaphoreType.DMA((19,)),
        ],
        compiler_params=pltpu.CompilerParams(vmem_limit_bytes=(51 if held else 56) * 2**20),
        cost_estimate=pl.CostEstimate(
            flops=4 * height * features * hidden, bytes_accessed=4 * (height + hidden) * features, transcendentals=0
        ),
    )(rows, kept, w_down, w_up)


def solution(mesh):
    return jax.shard_map(
        on_device,
        mesh=mesh,
        in_specs=(
            P("section", ("outer", "inner"), None),
            P("section", ("outer", "inner"), None),
            P("section", ("outer", "inner"), None),
            P("section", ("outer", "inner"), None, None),
            P("section", ("outer", "inner"), None, None),
            P("section", ("outer", "inner"), None, None),
        ),
        out_specs=(
            P("section", ("outer", "inner"), None),
            P("section", ("outer", "inner"), None, None),
        ),
        check_vma=False,
    )
```
